512 devices in a mesh: rep: 16 (over x, z_lo), fsdp: 32 (over z_hi, y, core).
Axes of the slice: x: 4, y: 8, z: 8 (z_hi: 2, z_lo: 4; z = z_hi * 4 + z_lo), core: 2. Of those that a mesh axis runs over, the one named last changes fastest.
Arguments:
- activations: bfloat16 [2048, 8192], P('fsdp', 'rep'), may hold values from -6 to 6
- out_grads: bfloat16 [2048, 32768], P('rep', 'fsdp'), may hold values from -0.19921875 to 0.19921875
- in_basis: bfloat16 [8192, 512], P('rep', 'fsdp'), may hold values from -0.25 to 0.25
- out_basis: bfloat16 [32768, 1024], P('fsdp', 'rep'), may hold values from -0.1875 to 0.1875
Outputs:
- scaled_grad: float32 [8192, 32768], P('rep', 'fsdp')
The draws below stay inside these ranges and needn't reach their ends.
All inputs are finite; a program needn't handle non-finite values.
Results may differ from the reference program's by a relative error of at most 0.0041.
Values may be sent and summed in bfloat16 or wider, within the bound.
A program may use at most 64 MiB of HBM per device.

```python
import jax
import jax.numpy as jnp

D = 8192
FF = 32768
BA = 512
BG = 1024
TOKENS = 2048


def shard_levels(own_key, dims, split, least, largest):
    def one(axis_at, blocks):
        draws = jax.random.uniform(jax.random.fold_in(jax.random.fold_in(own_key, 6), axis_at), (blocks,), jnp.float32, least / len(split), largest / len(split))
        return jnp.repeat(jnp.exp(draws), dims[axis_at] // blocks).reshape((-1,) + (1,) * (len(dims) - axis_at - 1))

    factor_of = one(*split[0])
    for cut in split[1:]:
        factor_of = factor_of * one(*cut)
    return factor_of


def bell_draw(rng, shape, scale, most, split=(), kind=jnp.bfloat16):
    array = jax.random.normal(rng, shape, jnp.float32) * scale
    if len(split) > 0:
        array = shard_levels(rng, shape, split, -0.22, 0.18) * array
    return jnp.clip(array, min=-most, max=most).astype(kind)


def setup_inputs(seed: int = 0) -> dict:
    seeds = jax.random.split(jax.random.key(seed), 5)
    return {
        "activations": bell_draw(seeds[0], (TOKENS, D), 1.0, 6.0, ((0, 32), (1, 16))),
        "out_grads": bell_draw(seeds[1], (TOKENS, FF), 0.03, 0.19921875, ((0, 16), (1, 32))),
        "in_basis": bell_draw(seeds[2], (D, BA), BA ** -0.5, 0.25, ((0, 16), (1, 32))),
        "out_basis": bell_draw(seeds[3], (FF, BG), BG ** -0.5, 0.1875, ((0, 32), (1, 16))),
    }


damping = 1e-3


def rotate(data, basis):
    count = data.shape[0]
    width = basis.shape[1]
    parts = data.astype(jnp.float32).reshape(count, -1, width)
    blocks = basis.astype(jnp.float32).reshape(-1, width, width)
    turned = jnp.einsum("tkb,kbc->tkc", parts, blocks)
    return turned.reshape(count, -1).astype(jnp.bfloat16)


def reference(activations, out_grads, in_basis, out_basis):
    rot_x = rotate(activations, in_basis)
    rot_g = rotate(out_grads, out_basis)
    sq_x = (rot_x.astype(jnp.float32) ** 2).astype(jnp.bfloat16)
    sq_g = (rot_g.astype(jnp.float32) ** 2).astype(jnp.bfloat16)
    scale_sum = jnp.dot(sq_x.T, sq_g, preferred_element_type=jnp.float32)
    grad_sum = jnp.dot(rot_x.T, rot_g, preferred_element_type=jnp.float32)
    return (grad_sum / TOKENS) / (scale_sum / TOKENS + damping)
```

```python
import functools

import jax
import jax.numpy as jnp
from jax import lax
from jax.experimental import pallas as pl
from jax.experimental.pallas import tpu as pltpu
from jax.sharding import PartitionSpec as P

MESH = pl.DeviceIdType.MESH
DAMPING = 0.001
TOKENS = 2048
NX, NL, NH, NY = 4, 4, 2, 8
ZROWS = 208
WROWS = 256 - ZROWS
XROWS = 80
NT = (((1,), (1,)), ((), ()))


def dot_nt(a, b):
    return lax.dot_general(a, b, NT, preferred_element_type=jnp.float32)


def square(a):
    wide = a.astype(jnp.float32)
    return (wide * wide).astype(jnp.bfloat16)


def slot_of(x):
    return (x % 2) * 2 + x // 2


def kernel(xb_ref, g_ref, bt_ref, o_ref, xbuf, gbuf, bbuf, rt, bx, rx, sx, send_sem, recv_sem):
    rep, f = lax.axis_index("rep"), lax.axis_index("fsdp")
    x, zl = rep // NL, rep % NL
    zh, y, c = f // 16, (f // 2) % NY, f % 2
    inner = (zl + 1) // 2 % 2 == 1
    xp = (((x + 1) % NX) * NL + zl, f)
    xm = (((x + 3) % NX) * NL + zl, f)
    first = zl + 1 - 2 * (zl % 2)
    nb1 = (x * NL + first, f)
    nb2 = (x * NL + (3 - zl), f)
    yp = (rep, zh * 16 + ((y + 1) % NY) * 2 + c)
    ym = (rep, zh * 16 + ((y + 7) % NY) * 2 + c)
    z4 = (rep, (1 - zh) * 16 + y * 2 + c)
    co = (rep, f + 1 - 2 * c)
    arrivals = (first, 2 - zl // 2, 3 - 3 * (zl // 2))

    sent = []
    ids = [0, 0]

    def new_recv(n=1):
        ids[1] += n
        return ids[1] - n

    def copy(src, dst, s, r, dev):
        return pltpu.make_async_remote_copy(
            src_ref=src, dst_ref=dst, send_sem=send_sem.at[s], recv_sem=recv_sem.at[r],
            device_id=dev, device_id_type=MESH)

    def send(src, dst, r, dev, cond=None):
        s = ids[0]
        ids[0] += 1
        cp = copy(src, dst, s, r, dev)
        if cond is None:
            cp.start()
        else:
            pl.when(cond)(cp.start)
        sent.append((cp, cond))

    def recv(dst, r):
        copy(dst, dst, 0, r, xp).wait_recv()

    barrier = pltpu.get_barrier_semaphore()
    for dev in (xp, xm, nb1, yp, ym, z4, co):
        pl.semaphore_signal(barrier, inc=1, device_id=dev, device_id_type=MESH)

    @pl.when(inner)
    def _():
        pl.semaphore_signal(barrier, inc=1, device_id=nb2, device_id_type=MESH)

    pl.semaphore_wait(barrier, 7 + (zl + 1) // 2 % 2)

    g_own, g_m, g_p, g_2 = (slot_of((x + d) % NX) for d in (0, 3, 1, 2))
    h0, h1 = pl.ds(0, 64), pl.ds(64, 64)
    r_g = new_recv(6)
    send(g_ref.at[h0], gbuf.at[g_own, h0], r_g, xp)
    send(g_ref.at[h1], gbuf.at[g_own, h1], r_g + 1, xm)
    r_b = new_recv(NL)
    send(bt_ref, bbuf.at[zl], r_b + zl, nb1)
    send(bt_ref, bbuf.at[zl], r_b + zl, nb2, inner)
    ys = [((y + d) % NY) % 4 * 2 + ((y + d) % NY) // 4 for d in range(NY)]
    r_zh, r_co = new_recv(), new_recv()
    send(xb_ref, xbuf.at[ys[0], zh, c], r_zh, z4)
    r_y = [[new_recv(2) for _ in range(4)] for _ in range(2)]
    r_c = [[new_recv(2) for _ in range(4)] for _ in range(2)]
    r_co2 = new_recv()
    send(xb_ref, xbuf.at[ys[0], zh, c], r_y[0][0], yp)
    send(xb_ref, xbuf.at[ys[0], zh, c], r_y[0][0] + 1, ym)
    send(xb_ref, xbuf.at[ys[0], zh, c], r_co, co)
    send(g_ref.at[h1], gbuf.at[g_own, h1], r_g + 2, xp)
    send(g_ref.at[h0], gbuf.at[g_own, h0], r_g + 3, xm)

    gbuf[g_own] = g_ref[...]
    bbuf[zl] = bt_ref[...]
    xbuf[ys[0], zh, c] = xb_ref[...]
    left, right = pl.ds(0, 256), pl.ds(256, 256)
    every = pl.ds(0, XROWS)

    def y_step(flow, k):
        hz = zh if flow == 0 else 1 - zh
        for way in range(2):
            src = xbuf.at[ys[(8 - k) % 8 if way == 0 else k], hz, c]
            to = yp if way == 0 else ym
            half = left if way == 0 else right
            r = r_y[flow][k - 1] + way
            if k == 4:
                src = src.at[every, half]
            recv(src, r)
            if k < 3:
                send(src, src, r_y[flow][k] + way, to)
            elif k == 3:
                send(src.at[every, half], src.at[every, half], r_y[flow][k] + way, to)
            send(src, src, r_c[flow][k - 1] + way, co)

    def y_core(flow, k):
        hz = zh if flow == 0 else 1 - zh
        for way in range(2):
            dst = xbuf.at[ys[(8 - k) % 8 if way == 0 else k], hz, 1 - c]
            if k == 4:
                dst = dst.at[every, left if way == 0 else right]
            recv(dst, r_c[flow][k - 1] + way)

    def b_event(e):
        s = arrivals[e]
        recv(bbuf.at[s], r_b + s)
        send(bbuf.at[s], bbuf.at[s], r_b + s, nb2 if e == 0 else nb1, inner)

    y_step(0, 1)
    b_event(0)
    recv(gbuf.at[g_m, h0], r_g)
    send(gbuf.at[g_m, h0], gbuf.at[g_m, h0], r_g + 4, xp)
    recv(gbuf.at[g_p, h1], r_g + 1)
    send(gbuf.at[g_p, h1], gbuf.at[g_p, h1], r_g + 5, xm)
    b_event(1)
    far = xbuf.at[ys[0], 1 - zh, c]
    recv(far, r_zh)
    send(far, far, r_y[1][0], yp)
    send(far, far, r_y[1][0] + 1, ym)
    send(far, far, r_co2, co)
    y_step(0, 2)
    b_event(2)
    y_step(1, 1)
    recv(gbuf.at[g_m, h1], r_g + 2)
    recv(gbuf.at[g_p, h0], r_g + 3)
    recv(gbuf.at[g_2, h0], r_g + 4)
    recv(gbuf.at[g_2, h1], r_g + 5)

    tile = dot_nt(bbuf[...].reshape(256, 1024), gbuf[...].reshape(512, 1024))
    rt[0, zl] = tile.astype(jnp.bfloat16)

    zrows, wrows = pl.ds(0, ZROWS), pl.ds(ZROWS, WROWS)
    r_t = new_recv(NL)
    r_w = new_recv(4)
    r_v = new_recv(NL)
    r_x = [new_recv(6) for _ in range(NL)]

    own = rt.at[0, zl]
    send(own.at[wrows], rt.at[3, zl, wrows], r_w, xp)
    send(own.at[wrows], rt.at[1, zl, wrows], r_w + 1, xm)
    send(own, own, r_t + zl, nb1)
    send(own, own, r_t + zl, nb2, inner)

    def x_sends(s, r):
        for first_half in (True, False):
            lp, lm = (left, right) if first_half else (right, left)
            k = 0 if first_half else 2
            send(rt.at[0, s, zrows, lp], rt.at[3, s, zrows, lp], r + k, xp)
            send(rt.at[0, s, zrows, lm], rt.at[1, s, zrows, lm], r + k + 1, xm)

    def x_forward(s, r):
        recv(rt.at[3, s, zrows, left], r)
        send(rt.at[3, s, zrows, left], rt.at[2, s, zrows, left], r + 4, xp)
        recv(rt.at[1, s, zrows, right], r + 1)
        send(rt.at[1, s, zrows, right], rt.at[2, s, zrows, right], r + 5, xm)

    def t_event(e):
        s = arrivals[e]
        recv(rt.at[0, s], r_t + s)
        send(rt.at[0, s], rt.at[0, s], r_t + s, nb2 if e == 0 else nb1, inner)

    def v_event(e):
        s = arrivals[e]
        part = rt.at[pl.ds(1, 3), s, wrows]
        recv(part, r_v + s)
        send(part, part, r_v + s, nb2 if e == 0 else nb1, inner)

    x_sends(zl, r_x[0])
    y_step(0, 3)
    y_step(1, 2)
    recv(rt.at[3, zl, wrows], r_w)
    send(rt.at[3, zl, wrows, left], rt.at[2, zl, wrows, left], r_w + 2, xp)
    recv(rt.at[1, zl, wrows], r_w + 1)
    send(rt.at[1, zl, wrows, right], rt.at[2, zl, wrows, right], r_w + 3, xm)
    y_step(0, 4)
    t_event(0)
    x_sends(arrivals[0], r_x[1])
    recv(rt.at[2, zl, wrows, left], r_w + 2)
    recv(rt.at[2, zl, wrows, right], r_w + 3)
    mine = rt.at[pl.ds(1, 3), zl, wrows]
    send(mine, mine, r_v + zl, nb1)
    send(mine, mine, r_v + zl, nb2, inner)
    x_forward(zl, r_x[0])
    t_event(1)
    x_sends(arrivals[1], r_x[2])
    y_step(1, 3)
    v_event(0)
    x_forward(arrivals[0], r_x[1])
    t_event(2)
    x_sends(arrivals[2], r_x[3])
    v_event(1)
    y_step(1, 4)
    x_forward(arrivals[1], r_x[2])

    recv(xbuf.at[ys[0], zh, 1 - c], r_co)
    recv(xbuf.at[ys[0], 1 - zh, 1 - c], r_co2)
    for flow in range(2):
        for k in range(1, 5):
            y_core(flow, k)
    for i in range(32):
        ih, iy, ic = i // 16, i // 2 % 8, i % 2
        bx[pl.ds(i * 16, 16), :] = xbuf[iy % 4 * 2 + iy // 4, ih, ic, pl.ds(64, 16), :]

    def rot_x(t, _):
        data = xbuf[pl.ds(t * 2, 2), :, :, pl.ds(0, 64), :].reshape(512, 512)
        turned = dot_nt(bx[...], data).astype(jnp.bfloat16)
        rx[t] = turned
        sx[t] = square(turned)
        return 0

    lax.fori_loop(0, NL, rot_x, 0)
    v_event(2)
    x_forward(arrivals[2], r_x[3])

    def columns(dx):
        col = pl.ds(pl.multiple_of((x + dx) % NX * 256, 256), 256)

        def rows(m, _):
            here = pl.ds(pl.multiple_of(m * 256, 256), 256)
            grad = jnp.zeros((256, 256), jnp.float32)
            scale = jnp.zeros((256, 256), jnp.float32)
            for t in range(NL):
                piece = rt[dx, t]
                grad += dot_nt(rx[t, here, :], piece)
                scale += dot_nt(sx[t, here, :], square(piece))
            o_ref[here, col] = (grad / TOKENS) / (scale / TOKENS + DAMPING)
            return 0

        lax.fori_loop(0, 2, rows, 0)

    slots = (zl,) + arrivals
    columns(0)
    for i in range(NL):
        recv(rt.at[1, slots[i], zrows, left], r_x[i] + 3)
    columns(1)
    for i in range(NL):
        recv(rt.at[3, slots[i], zrows, right], r_x[i] + 2)
    columns(3)
    for i in range(NL):
        recv(rt.at[2, slots[i], zrows, left], r_x[i] + 4)
        recv(rt.at[2, slots[i], zrows, right], r_x[i] + 5)
    columns(2)

    for cp, cond in sent:
        if cond is None:
            cp.wait_send()
        else:
            pl.when(cond)(cp.wait_send)


def per_device(activations, out_grads, in_basis, out_basis):
    xb = jnp.concatenate([activations, in_basis.T], axis=0)
    bf = jnp.bfloat16
    vmem = pl.BlockSpec(memory_space=pltpu.VMEM)
    return pl.pallas_call(
        kernel,
        out_shape=jax.ShapeDtypeStruct((512, 1024), jnp.float32),
        in_specs=[vmem] * 3,
        out_specs=vmem,
        scratch_shapes=[
            pltpu.VMEM((NY, NH, 2, XROWS, 512), bf),
            pltpu.VMEM((NX, 128, 1024), bf),
            pltpu.VMEM((NL, 64, 1024), bf),
            pltpu.VMEM((NX, NL, 256, 512), bf),
            pltpu.VMEM((512, 512), bf),
            pltpu.VMEM((NL, 512, 512), bf),
            pltpu.VMEM((NL, 512, 512), bf),
            pltpu.SemaphoreType.DMA((100,)),
            pltpu.SemaphoreType.DMA((100,)),
        ],
        compiler_params=pltpu.CompilerParams(
            collective_id=0, has_side_effects=True, vmem_limit_bytes=48 * 2**20),
        cost_estimate=pl.CostEstimate(
            flops=6 * 10**9, bytes_accessed=4 * 2**20, transcendentals=0),
        name="gather_and_scale",
    )(xb, out_grads, out_basis.T)


def solution(mesh):
    in_specs = (P("fsdp", "rep"), P("rep", "fsdp"), P("rep", "fsdp"), P("fsdp", "rep"))
    out_specs = P("rep", "fsdp")
    return jax.shard_map(
        per_device, mesh=mesh, in_specs=in_specs, out_specs=out_specs, check_vma=False
    )
```

```python
import functools

import jax
import jax.numpy as jnp
from jax import lax
from jax.experimental import pallas as pl
from jax.experimental.pallas import tpu as pltpu
from jax.sharding import PartitionSpec as P

MESH = pl.DeviceIdType.MESH
DAMPING = 0.001
TOKENS = 2048
NX, NL, NH, NY = 4, 4, 2, 8
ZROWS = 208
WROWS = 256 - ZROWS
XROWS = 80
NT = (((1,), (1,)), ((), ()))


def dot_nt(a, b):
    return lax.dot_general(a, b, NT, preferred_element_type=jnp.float32)


def square(a):
    wide = a.astype(jnp.float32)
    return (wide * wide).astype(jnp.bfloat16)


def slot_of(x):
    return (x % 2) * 2 + x // 2


def kernel(x_ref, i_ref, g_ref, bt_ref, o_ref, xbuf, gbuf, bbuf, rt, bx, rx, sx, send_sem, recv_sem, own_sem):
    rep, f = lax.axis_index("rep"), lax.axis_index("fsdp")
    x, zl = rep // NL, rep % NL
    zh, y, c = f // 16, (f // 2) % NY, f % 2
    inner = (zl + 1) // 2 % 2 == 1
    xp = (((x + 1) % NX) * NL + zl, f)
    xm = (((x + 3) % NX) * NL + zl, f)
    x2 = (((x + 2) % NX) * NL + zl, f)
    first = zl + 1 - 2 * (zl % 2)
    arrivals = (first, 2 - zl // 2, 3 - 3 * (zl // 2))
    line = [(x * NL + s, f) for s in arrivals]
    nb1 = line[0]
    nb2 = (x * NL + (3 - zl), f)
    yd = [(rep, zh * 16 + ((y + d) % NY) * 2 + c) for d in range(NY)]
    z4 = (rep, (1 - zh) * 16 + y * 2 + c)
    co = (rep, f + 1 - 2 * c)

    sent = []
    ids = [0, 0]

    def new_recv(n=1):
        ids[1] += n
        return ids[1] - n

    def copy(src, dst, s, r, dev):
        return pltpu.make_async_remote_copy(
            src_ref=src, dst_ref=dst, send_sem=send_sem.at[s], recv_sem=recv_sem.at[r],
            device_id=dev, device_id_type=MESH)

    def send(src, dst, r, dev, cond=None):
        s = ids[0]
        ids[0] += 1
        cp = copy(src, dst, s, r, dev)
        if cond is None:
            cp.start()
        else:
            pl.when(cond)(cp.start)
        sent.append((cp, cond))

    def pass_on(ref, r, dev, cond=None):
        send(ref, ref, r, dev, cond)

    def recv(dst, r):
        copy(dst, dst, 0, r, xp).wait_recv()

    barrier = pltpu.get_barrier_semaphore()
    partners = [xp, xm, x2, *line, yd[1], yd[7], yd[2], yd[6], z4, co]
    for dev in partners:
        pl.semaphore_signal(barrier, inc=1, device_id=dev, device_id_type=MESH)

    ys = [((y + d) % NY) % 4 * 2 + ((y + d) % NY) // 4 for d in range(NY)]
    g_own, g_m, g_p, g_2 = (slot_of((x + d) % NX) for d in (0, 3, 1, 2))
    x_own = xbuf.at[ys[0], zh, c]
    load = [
        pltpu.make_async_copy(g_ref, gbuf.at[g_own], own_sem.at[0]),
        pltpu.make_async_copy(bt_ref, bbuf.at[zl], own_sem.at[1]),
        pltpu.make_async_copy(x_ref, x_own.at[pl.ds(0, 64)], own_sem.at[2]),
        pltpu.make_async_copy(i_ref, x_own.at[pl.ds(64, 16)], own_sem.at[3]),
    ]
    for cp in load:
        cp.start()
    for cp in load:
        cp.wait()
    pl.semaphore_wait(barrier, len(partners))

    left, right = pl.ds(0, 256), pl.ds(256, 256)
    h0, h1 = pl.ds(0, 64), pl.ds(64, 64)
    every = pl.ds(0, XROWS)

    r_g = new_recv(6)
    pass_on(gbuf.at[g_own, h0], r_g, xp)
    pass_on(gbuf.at[g_own, h1], r_g + 1, xm)
    r_b = new_recv(NL)
    for dev in line:
        pass_on(bbuf.at[zl], r_b + zl, dev)
    pass_on(gbuf.at[g_own, h1], r_g + 2, xp)
    pass_on(gbuf.at[g_own, h0], r_g + 3, xm)
    r_zh = new_recv()
    pass_on(x_own, r_zh, z4)
    r_near = [[new_recv() for _ in range(4)] for _ in range(2)]
    near = (1, 7, 2, 6)

    def x_near(flow):
        piece = xbuf.at[ys[0], zh if flow == 0 else 1 - zh, c]
        for k, d in enumerate(near):
            pass_on(piece, r_near[flow][k], yd[d])

    x_near(0)

    recv(gbuf.at[g_m, h0], r_g)
    pass_on(gbuf.at[g_m, h0], r_g + 4, xp)
    recv(gbuf.at[g_p, h1], r_g + 1)
    pass_on(gbuf.at[g_p, h1], r_g + 5, xm)
    recv(xbuf.at[ys[0], 1 - zh, c], r_zh)
    x_near(1)
    r_core = [new_recv() for _ in range(9)]
    pass_on(xbuf.at[ys[0], :, c], r_core[0], co)
    recv(gbuf.at[g_m, h1], r_g + 2)
    recv(gbuf.at[g_p, h0], r_g + 3)
    recv(gbuf.at[g_2, h0], r_g + 4)
    recv(gbuf.at[g_2, h1], r_g + 5)
    for s in arrivals:
        recv(bbuf.at[s], r_b + s)

    tile = dot_nt(bbuf[...].reshape(256, 1024), gbuf[...].reshape(512, 1024))
    rt[0, zl] = tile.astype(jnp.bfloat16)

    zrows, wrows = pl.ds(0, ZROWS), pl.ds(ZROWS, WROWS)
    r_t = new_recv(NL)
    r_w = new_recv(3)
    r_v = new_recv(NL)
    r_x = [new_recv(6) for _ in range(NL)]

    def x_sends(s, r, first_half):
        lp, lm = (left, right) if first_half else (right, left)
        k = 0 if first_half else 2
        send(rt.at[0, s, zrows, lp], rt.at[3, s, zrows, lp], r + k, xp)
        send(rt.at[0, s, zrows, lm], rt.at[1, s, zrows, lm], r + k + 1, xm)

    def x_forward(s, r):
        recv(rt.at[3, s, zrows, left], r)
        send(rt.at[3, s, zrows, left], rt.at[2, s, zrows, left], r + 4, xp)
        recv(rt.at[1, s, zrows, right], r + 1)
        send(rt.at[1, s, zrows, right], rt.at[2, s, zrows, right], r + 5, xm)

    def t_event(e):
        s = arrivals[e]
        recv(rt.at[0, s], r_t + s)
        pass_on(rt.at[0, s], r_t + s, nb2 if e == 0 else nb1, inner)
        x_sends(s, r_x[e + 1], True)
        x_sends(s, r_x[e + 1], False)

    own = rt.at[0, zl]
    x_sends(zl, r_x[0], True)
    pass_on(own, r_t + zl, nb1)
    pass_on(own, r_t + zl, nb2, inner)
    x_sends(zl, r_x[0], False)
    send(own.at[wrows], rt.at[3, zl, wrows], r_w, xp)
    send(own.at[wrows], rt.at[1, zl, wrows], r_w + 1, xm)
    send(own.at[wrows], rt.at[2, zl, wrows], r_w + 2, x2)

    x_forward(zl, r_x[0])
    r_far = [new_recv() for _ in range(4)]
    for flow in range(2):
        hz = zh if flow == 0 else 1 - zh
        for k, d in enumerate(near):
            recv(xbuf.at[ys[(8 - d) % 8], hz, c], r_near[flow][k])
    for way in range(2):
        piece = xbuf.at[ys[6 if way == 0 else 2], :, c]
        pass_on(piece, r_far[way], yd[1 if way == 0 else 7])
        half = xbuf.at[ys[6 if way == 0 else 2], way, c]
        pass_on(half, r_far[2 + way], yd[2 if way == 0 else 6])
    for k, d in enumerate(near):
        pass_on(xbuf.at[ys[d], :, c], r_core[1 + k], co)

    t_event(0)
    for d, slot in enumerate((3, 1, 2)):
        recv(rt.at[slot, zl, wrows], r_w + d)
    mine = rt.at[pl.ds(1, 3), zl, wrows]
    for dev in line:
        pass_on(mine, r_v + zl, dev)
    x_forward(arrivals[0], r_x[1])
    t_event(1)
    x_forward(arrivals[1], r_x[2])
    for way in range(2):
        recv(xbuf.at[ys[5 if way == 0 else 3], :, c], r_far[way])
        recv(xbuf.at[ys[4], way, c], r_far[2 + way])
    for k, d in enumerate((3, 5, 4)):
        pass_on(xbuf.at[ys[d], :, c], r_core[5 + k], co)
    t_event(2)

    for k, d in enumerate((0,) + near + (3, 5, 4)):
        recv(xbuf.at[ys[d], :, 1 - c], r_core[k])
    for i in range(32):
        ih, iy, ic = i // 16, i // 2 % 8, i % 2
        bx[pl.ds(i * 16, 16), :] = xbuf[iy % 4 * 2 + iy // 4, ih, ic, pl.ds(64, 16), :]

    def rot_x(t, _):
        data = xbuf[pl.ds(t * 2, 2), :, :, pl.ds(0, 64), :].reshape(512, 512)
        turned = dot_nt(bx[...], data).astype(jnp.bfloat16)
        rx[t] = turned
        sx[t] = square(turned)
        return 0

    lax.fori_loop(0, NL, rot_x, 0)
    x_forward(arrivals[2], r_x[3])

    def columns(dx):
        col = pl.ds(pl.multiple_of((x + dx) % NX * 256, 256), 256)

        def rows(m, _):
            here = pl.ds(pl.multiple_of(m * 256, 256), 256)
            grad = jnp.zeros((256, 256), jnp.float32)
            scale = jnp.zeros((256, 256), jnp.float32)
            for t in range(NL):
                piece = rt[dx, t]
                grad += dot_nt(rx[t, here, :], piece)
                scale += dot_nt(sx[t, here, :], square(piece))
            o_ref[here, col] = (grad / TOKENS) / (scale / TOKENS + DAMPING)
            return 0

        lax.fori_loop(0, 2, rows, 0)

    slots = (zl,) + arrivals
    columns(0)
    for s in arrivals:
        recv(rt.at[pl.ds(1, 3), s, wrows], r_v + s)
    for i in range(NL):
        recv(rt.at[1, slots[i], zrows, left], r_x[i] + 3)
    columns(1)
    for i in range(NL):
        recv(rt.at[3, slots[i], zrows, right], r_x[i] + 2)
    columns(3)
    for i in range(NL):
        recv(rt.at[2, slots[i], zrows, left], r_x[i] + 4)
        recv(rt.at[2, slots[i], zrows, right], r_x[i] + 5)
    columns(2)

    for cp, cond in sent:
        if cond is None:
            cp.wait_send()
        else:
            pl.when(cond)(cp.wait_send)


def per_device(activations, out_grads, in_basis, out_basis):
    bf = jnp.bfloat16
    vmem = pl.BlockSpec(memory_space=pltpu.VMEM)
    return pl.pallas_call(
        kernel,
        out_shape=jax.ShapeDtypeStruct((512, 1024), jnp.float32),
        in_specs=[pl.BlockSpec(memory_space=pltpu.HBM)] * 4,
        out_specs=vmem,
        scratch_shapes=[
            pltpu.VMEM((NY, NH, 2, XROWS, 512), bf),
            pltpu.VMEM((NX, 128, 1024), bf),
            pltpu.VMEM((NL, 64, 1024), bf),
            pltpu.VMEM((NX, NL, 256, 512), bf),
            pltpu.VMEM((512, 512), bf),
            pltpu.VMEM((NL, 512, 512), bf),
            pltpu.VMEM((NL, 512, 512), bf),
            pltpu.SemaphoreType.DMA((100,)),
            pltpu.SemaphoreType.DMA((100,)),
            pltpu.SemaphoreType.DMA((4,)),
        ],
        compiler_params=pltpu.CompilerParams(
            collective_id=0, has_side_effects=True, vmem_limit_bytes=48 * 2**20),
        cost_estimate=pl.CostEstimate(
            flops=6 * 10**9, bytes_accessed=4 * 2**20, transcendentals=0),
        name="gather_and_scale",
    )(activations, in_basis.T, out_grads, out_basis.T)


def solution(mesh):
    in_specs = (P("fsdp", "rep"), P("rep", "fsdp"), P("rep", "fsdp"), P("fsdp", "rep"))
    out_specs = P("rep", "fsdp")
    return jax.shard_map(
        per_device, mesh=mesh, in_specs=in_specs, out_specs=out_specs, check_vma=False
    )
```

```python
import functools

import jax
import jax.numpy as jnp
from jax import lax
from jax.experimental import pallas as pl
from jax.experimental.pallas import tpu as pltpu
from jax.sharding import PartitionSpec as P

MESH = pl.DeviceIdType.MESH
DAMPING = 0.001
TOKENS = 2048
NX, NL, NH, NY = 4, 4, 2, 8
XROWS = 80
WROWS = 32
A_ROWS = pl.ds(0, 128)
B_ROWS = pl.ds(128, 128)
BZ_ROWS = pl.ds(128, 128 - WROWS)
W_ROWS = pl.ds(256 - WROWS, WROWS)
LEFT, RIGHT = pl.ds(0, 256), pl.ds(256, 256)
NT = (((1,), (1,)), ((), ()))
END_ORDER = (
    "Z4", "B0", "G2", "Y01", "G1", "GA", "XZ", "B1", "B2", "GB", "Y02", "WX", "Y11", "T0A",
    "WF", "T0B", "Y12", "Y03", "T1A", "F1A", "WZ", "F0B", "T1B", "Y04", "F0A", "Y13", "T2A",
    "Y14", "T2B", "F1B", "RX", "V1", "F2B", "V0", "V2", "F2A", "C0", "F3B", "F3A",
)
INNER_ORDER = (
    "B1", "B0", "G1", "G2", "Z4", "Y01", "B2", "GA", "GB", "Y02", "XZ", "WX", "T0A", "T1A",
    "Y03", "WF", "Y11", "T1B", "T0B", "T2A", "F1A", "F0B", "Y12", "Y04", "T2B", "WZ", "V0",
    "Y13", "F0A", "V1", "F1B", "F2B", "Y14", "F2A", "F3A", "V2", "RX", "F3B", "C0",
)


def dot_nt(a, b):
    return lax.dot_general(a, b, NT, preferred_element_type=jnp.float32)


def square(a):
    wide = a.astype(jnp.float32)
    return (wide * wide).astype(jnp.bfloat16)


def slot_of(x):
    return (x % 2) * 2 + x // 2


def along_plus(i, h):
    return (h + i) % 2 == 0


def kernel(x_ref, i_ref, g_ref, bt_ref, o_ref, out, xbuf, gbuf, bbuf, rt, bx, rx, sx, send_sem, recv_sem, own_sem, out_sem):
    rep, f = lax.axis_index("rep"), lax.axis_index("fsdp")
    x, zl = rep // NL, rep % NL
    zh, y, c = f // 16, (f // 2) % NY, f % 2
    inner = (zl + 1) // 2 % 2
    xp = (((x + 1) % NX) * NL + zl, f)
    xm = (((x + 3) % NX) * NL + zl, f)
    arrivals = (zl + 1 - 2 * (zl % 2), 2 - zl // 2, 3 - 3 * (zl // 2))
    slots = (zl,) + arrivals
    nb1 = (x * NL + arrivals[0], f)
    nb2 = (x * NL + (3 - zl), f)
    yp = (rep, zh * 16 + ((y + 1) % NY) * 2 + c)
    ym = (rep, zh * 16 + ((y + 7) % NY) * 2 + c)
    z4 = (rep, (1 - zh) * 16 + y * 2 + c)
    co = (rep, f + 1 - 2 * c)
    ys = [((y + d) % NY) % 4 * 2 + ((y + d) % NY) // 4 for d in range(NY)]
    g_own, g_m, g_p, g_2 = (slot_of((x + d) % NX) for d in (0, 3, 1, 2))
    pair = zl // 2 * 2
    hzs = (zh, 1 - zh)

    count = [0]

    def sems(n):
        count[0] += n
        return count[0] - n

    r_g, r_b, r_zh = sems(6), sems(2 * NL), sems(1)
    r_y, r_c, r_co = sems(16), sems(16), sems(2)
    r_t, r_x, r_f = sems(2 * NL), sems(4 * NL), sems(2 * NL)
    r_w, r_v = sems(4), sems(NL)

    def copy(src, dst, s, r, dev):
        return pltpu.make_async_remote_copy(
            src_ref=src, dst_ref=dst, send_sem=send_sem.at[s], recv_sem=recv_sem.at[r],
            device_id=dev, device_id_type=MESH)

    def arrived(dst, r):
        copy(dst, dst, 0, r, xp).wait_recv()

    barrier = pltpu.get_barrier_semaphore()
    for dev in (xp, xm, nb1, yp, ym, z4, co):
        pl.semaphore_signal(barrier, inc=1, device_id=dev, device_id_type=MESH)

    @pl.when(inner == 1)
    def _():
        pl.semaphore_signal(barrier, inc=1, device_id=nb2, device_id_type=MESH)

    x_own = xbuf.at[ys[0], zh, c]
    load = [
        pltpu.make_async_copy(g_ref, gbuf.at[g_own], own_sem.at[0]),
        pltpu.make_async_copy(bt_ref, bbuf.at[zl], own_sem.at[1]),
        pltpu.make_async_copy(x_ref, x_own.at[pl.ds(0, 64)], own_sem.at[2]),
        pltpu.make_async_copy(i_ref, x_own.at[pl.ds(64, 16)], own_sem.at[3]),
    ]
    for cp in load:
        cp.start()
    for cp in load:
        cp.wait()
    pl.semaphore_wait(barrier, 7 + inner)

    def rot_x(t, _):
        data = xbuf[pl.ds(t * 2, 2), :, :, pl.ds(0, 64), :].reshape(512, 512)
        turned = dot_nt(bx[...], data).astype(jnp.bfloat16)
        rx[t] = turned
        sx[t] = square(turned)
        return 0

    def columns(dx):
        col = pl.ds(pl.multiple_of((x + dx) % NX * 256, 256), 256)

        def rows(m, _):
            here = pl.ds(pl.multiple_of(m * 256, 256), 256)
            grad = jnp.zeros((256, 256), jnp.float32)
            scale = jnp.zeros((256, 256), jnp.float32)
            for t in range(NL):
                halves = [rt[dx, t, A_ROWS, :], rt[dx, t, B_ROWS, :]]
                piece = jnp.concatenate(halves if t < 2 else halves[::-1], axis=0)
                grad += dot_nt(rx[t, here, :], piece)
                scale += dot_nt(sx[t, here, :], square(piece))
            out[here, col] = (grad / TOKENS) / (scale / TOKENS + DAMPING)
            return 0

        lax.fori_loop(0, 2, rows, 0)
        return pltpu.make_async_copy(out.at[:, col], o_ref.at[:, col], out_sem.at[dx])

    def program(inside, order, finish):
        count = [0]

        def send(src, dst, r, dev):
            cp = copy(src, dst, count[0], r, dev)
            count[0] += 1
            if finish:
                cp.wait_send()
            else:
                cp.start()

        def recv(dst, r):
            if not finish:
                arrived(dst, r)

        def pass_on(ref, r, dev):
            send(ref, ref, r, dev)

        def own_z(ref, r):
            pass_on(ref, r, nb1)
            if inside:
                pass_on(ref, r, nb2)

        def next_z(e, ref, r):
            if inside:
                pass_on(ref, r, nb2 if e == 0 else nb1)

        def b_part(s, q):
            return bbuf.at[s, :, pl.ds(q * 512, 512)]

        def x_sends(i, h):
            s, r = slots[i], r_x + 4 * i + 2 * h
            rows = BZ_ROWS if h else A_ROWS
            send(rt.at[0, s, rows], rt.at[3, s, rows], r, xp)
            send(rt.at[0, s, rows], rt.at[1, s, rows], r + 1, xm)

        def tile(h):
            first = pair if h == 0 else 2 - pair
            rows = B_ROWS if h else A_ROWS
            if not finish:
                basis = bbuf[pl.ds(first, 2)].reshape(128, 1024)
                turned = dot_nt(basis, gbuf[...].reshape(512, 1024))
                rt[0, zl, rows, :] = turned.astype(jnp.bfloat16)
            own_z(rt.at[0, zl, rows], r_t + 2 * zl + h)
            x_sends(0, h)

        def y_event(flow, k):
            for way in range(2):
                src = xbuf.at[ys[(8 - k) % 8 if way == 0 else k], hzs[flow], c]
                to = yp if way == 0 else ym
                half = src.at[pl.ds(0, XROWS), LEFT if way == 0 else RIGHT]
                if k == 4:
                    src = half
                r = (flow * 4 + k - 1) * 2 + way
                recv(src, r_y + r)
                if k < 3:
                    pass_on(src, r_y + r + 2, to)
                elif k == 3:
                    pass_on(half, r_y + r + 2, to)
                pass_on(src, r_c + r, co)

        def event(name):
            kind = name[0]
            if name == "Z4":
                pass_on(x_own, r_zh, z4)
            elif name == "XZ":
                far = xbuf.at[ys[0], 1 - zh, c]
                recv(far, r_zh)
                pass_on(far, r_y + 8, yp)
                pass_on(far, r_y + 9, ym)
                pass_on(far, r_co + 1, co)
            elif kind == "Y":
                y_event(int(name[1]), int(name[2]))
            elif kind == "B":
                e = int(name[1])
                s = arrivals[e]
                for q in range(2):
                    recv(b_part(s, q), r_b + 2 * s + q)
                    next_z(e, b_part(s, q), r_b + 2 * s + q)
            elif name == "G1":
                recv(gbuf.at[g_m, h0], r_g)
                pass_on(gbuf.at[g_m, h0], r_g + 4, xp)
            elif name == "G2":
                recv(gbuf.at[g_p, h1], r_g + 1)
                pass_on(gbuf.at[g_p, h1], r_g + 5, xm)
            elif name == "GA":
                recv(gbuf.at[g_m, h1], r_g + 2)
                recv(gbuf.at[g_p, h0], r_g + 3)
                recv(gbuf.at[g_2, h0], r_g + 4)
                recv(gbuf.at[g_2, h1], r_g + 5)
                tile(0)
            elif name == "GB":
                tile(1)
            elif name == "WX":
                send(rt.at[0, zl, W_ROWS], rt.at[3, zl, W_ROWS], r_w, xp)
                send(rt.at[0, zl, W_ROWS], rt.at[1, zl, W_ROWS], r_w + 1, xm)
            elif name == "WF":
                recv(rt.at[3, zl, W_ROWS], r_w)
                send(rt.at[3, zl, W_ROWS, LEFT], rt.at[2, zl, W_ROWS, LEFT], r_w + 2, xp)
                recv(rt.at[1, zl, W_ROWS], r_w + 1)
                send(rt.at[1, zl, W_ROWS, RIGHT], rt.at[2, zl, W_ROWS, RIGHT], r_w + 3, xm)
            elif name == "WZ":
                recv(rt.at[2, zl, W_ROWS, LEFT], r_w + 2)
                recv(rt.at[2, zl, W_ROWS, RIGHT], r_w + 3)
                own_z(rt.at[pl.ds(1, 3), zl, W_ROWS], r_v + zl)
            elif kind == "V":
                e = int(name[1])
                s = arrivals[e]
                part = rt.at[pl.ds(1, 3), s, W_ROWS]
                recv(part, r_v + s)
                next_z(e, part, r_v + s)
            elif kind == "T":
                e, h = int(name[1]), "AB".index(name[2])
                s = arrivals[e]
                part = rt.at[0, s, B_ROWS if h else A_ROWS]
                recv(part, r_t + 2 * s + h)
                next_z(e, part, r_t + 2 * s + h)
                x_sends(e + 1, h)
            elif kind == "F":
                i, h = int(name[1]), "AB".index(name[2])
                s, rows, r = slots[i], BZ_ROWS if h else A_ROWS, r_x + 4 * i + 2 * h
                if along_plus(i, h):
                    recv(rt.at[3, s, rows], r)
                    send(rt.at[3, s, rows], rt.at[2, s, rows], r_f + 2 * i + h, xp)
                else:
                    recv(rt.at[1, s, rows], r + 1)
                    send(rt.at[1, s, rows], rt.at[2, s, rows], r_f + 2 * i + h, xm)
            elif finish:
                pass
            elif name == "RX":
                for flow in range(2):
                    recv(xbuf.at[ys[0], hzs[flow], 1 - c], r_co + flow)
                    for k in range(1, 5):
                        for way in range(2):
                            dst = xbuf.at[ys[(8 - k) % 8 if way == 0 else k], hzs[flow], 1 - c]
                            if k == 4:
                                dst = dst.at[pl.ds(0, XROWS), LEFT if way == 0 else RIGHT]
                            recv(dst, r_c + (flow * 4 + k - 1) * 2 + way)
                for i in range(32):
                    ih, iy, ic = i // 16, i // 2 % 8, i % 2
                    bx[pl.ds(i * 16, 16), :] = xbuf[iy % 4 * 2 + iy // 4, ih, ic, pl.ds(64, 16), :]
                lax.fori_loop(0, NL, rot_x, 0)
            elif name == "C0":
                columns(0).start()

        h0, h1 = pl.ds(0, 64), pl.ds(64, 64)
        pass_on(gbuf.at[g_own, h0], r_g, xp)
        pass_on(gbuf.at[g_own, h1], r_g + 1, xm)
        for q in range(2):
            own_z(b_part(zl, q), r_b + 2 * zl + q)
        pass_on(x_own, r_y, yp)
        pass_on(x_own, r_y + 1, ym)
        pass_on(x_own, r_co, co)
        pass_on(gbuf.at[g_own, h1], r_g + 2, xp)
        pass_on(gbuf.at[g_own, h0], r_g + 3, xm)
        for name in order:
            event(name)

    def both(finish):
        pl.when(inner == 0)(lambda: program(False, END_ORDER, finish))
        pl.when(inner == 1)(lambda: program(True, INNER_ORDER, finish))

    both(False)
    outs = []
    for i in range(NL):
        for h in range(2):
            if along_plus(i, h):
                arrived(rt.at[1, slots[i], BZ_ROWS if h else A_ROWS], r_x + 4 * i + 2 * h + 1)
    outs.append(columns(1))
    outs[-1].start()
    for i in range(NL):
        for h in range(2):
            if not along_plus(i, h):
                arrived(rt.at[3, slots[i], BZ_ROWS if h else A_ROWS], r_x + 4 * i + 2 * h)
    outs.append(columns(3))
    outs[-1].start()
    for i in range(NL):
        for h in range(2):
            arrived(rt.at[2, slots[i], BZ_ROWS if h else A_ROWS], r_f + 2 * i + h)
    outs.append(columns(2))
    outs[-1].start()

    both(True)
    col = pl.ds(pl.multiple_of(x * 256, 256), 256)
    outs.append(pltpu.make_async_copy(out.at[:, col], o_ref.at[:, col], out_sem.at[0]))
    for cp in outs:
        cp.wait()


def per_device(activations, out_grads, in_basis, out_basis):
    bf = jnp.bfloat16
    hbm = pl.BlockSpec(memory_space=pl.ANY)
    return pl.pallas_call(
        kernel,
        out_shape=jax.ShapeDtypeStruct((512, 1024), jnp.float32),
        in_specs=[hbm] * 4,
        out_specs=hbm,
        scratch_shapes=[
            pltpu.VMEM((512, 1024), jnp.float32),
            pltpu.VMEM((NY, NH, 2, XROWS, 512), bf),
            pltpu.VMEM((NX, 128, 1024), bf),
            pltpu.VMEM((NL, 64, 1024), bf),
            pltpu.VMEM((NX, NL, 256, 512), bf),
            pltpu.VMEM((512, 512), bf),
            pltpu.VMEM((NL, 512, 512), bf),
            pltpu.VMEM((NL, 512, 512), bf),
            pltpu.SemaphoreType.DMA((110,)),
            pltpu.SemaphoreType.DMA((100,)),
            pltpu.SemaphoreType.DMA((4,)),
            pltpu.SemaphoreType.DMA((4,)),
        ],
        compiler_params=pltpu.CompilerParams(
            collective_id=0, has_side_effects=True, vmem_limit_bytes=60 * 2**20),
        cost_estimate=pl.CostEstimate(
            flops=6 * 10**9, bytes_accessed=4 * 2**20, transcendentals=0),
        name="gather_and_scale",
    )(activations, in_basis.T, out_grads, out_basis.T)


def solution(mesh):
    in_specs = (P("fsdp", "rep"), P("rep", "fsdp"), P("rep", "fsdp"), P("fsdp", "rep"))
    out_specs = P("rep", "fsdp")
    return jax.shard_map(
        per_device, mesh=mesh, in_specs=in_specs, out_specs=out_specs, check_vma=False
    )
```

```python
import functools

import jax
import jax.numpy as jnp
from jax import lax
from jax.experimental import pallas as pl
from jax.experimental.pallas import tpu as pltpu
from jax.sharding import PartitionSpec as P

MESH = pl.DeviceIdType.MESH
DAMPING = 0.001
TOKENS = 2048
NX, NL, NH, NY = 4, 4, 2, 8
XROWS = 80
WROWS = 32
A_ROWS = pl.ds(0, 128)
B_ROWS = pl.ds(128, 128)
BZ_ROWS = pl.ds(128, 128 - WROWS)
W_ROWS = pl.ds(256 - WROWS, WROWS)
LEFT, RIGHT = pl.ds(0, 256), pl.ds(256, 256)
NT = (((1,), (1,)), ((), ()))
END_ORDER = (
    "L1", "L2", "G1", "L3", "Z4", "Y01", "G2", "B0", "GA", "B1", "B2", "GB", "WX", "XZ", "Y02",
    "T0A", "Y11", "WF", "T0B", "Y03", "T1A", "WZ", "Y12", "T1B", "Y04", "Y13", "F1A", "F2A",
    "F0B", "Y14", "T2A", "T2B", "F2B", "F1B", "F0A", "RX", "C0", "F3B", "V1", "V2", "V0", "F3A",
)
INNER_ORDER = (
    "L1", "L2", "B1", "B0", "L3", "Z4", "G2", "G1", "B2", "GA", "GB", "Y01", "XZ", "WX", "T1A",
    "T0A", "Y02", "Y11", "WF", "T0B", "T1B", "Y03", "T2A", "F0A", "Y12", "T2B", "WZ", "Y13",
    "F1B", "V0", "F0B", "F1A", "Y04", "F2B", "Y14", "V1", "F2A", "V2", "RX", "C0", "F3A", "F3B",
)


def dot_nt(a, b):
    return lax.dot_general(a, b, NT, preferred_element_type=jnp.float32)


def square(a):
    wide = a.astype(jnp.float32)
    return (wide * wide).astype(jnp.bfloat16)


def slot_of(x):
    return (x % 2) * 2 + x // 2


def along_plus(i, h):
    return (h + i) % 2 == 0


def kernel(own_ref, out, xbuf, gbuf, bbuf, rt, bx, rx, sx, acc, send_sem, recv_sem, own_sem, level):
    rep, f = lax.axis_index("rep"), lax.axis_index("fsdp")
    x, zl = rep // NL, rep % NL
    zh, y, c = f // 16, (f // 2) % NY, f % 2
    inner = (zl + 1) // 2 % 2
    xp = (((x + 1) % NX) * NL + zl, f)
    xm = (((x + 3) % NX) * NL + zl, f)
    arrivals = (zl + 1 - 2 * (zl % 2), 2 - zl // 2, 3 - 3 * (zl // 2))
    slots = (zl,) + arrivals
    nb1 = (x * NL + arrivals[0], f)
    nb2 = (x * NL + (3 - zl), f)
    z = zh * NL + zl
    zp, zm = (
        (x * NL + (z + d) % 8 % NL, (z + d) % 8 // NL * 16 + y * 2 + c) for d in (1, 7))
    yp = (rep, zh * 16 + ((y + 1) % NY) * 2 + c)
    ym = (rep, zh * 16 + ((y + 7) % NY) * 2 + c)
    z4 = (rep, (1 - zh) * 16 + y * 2 + c)
    co = (rep, f + 1 - 2 * c)
    ys = [((y + d) % NY) % 4 * 2 + ((y + d) % NY) // 4 for d in range(NY)]
    g_own, g_m, g_p, g_2 = (slot_of((x + d) % NX) for d in (0, 3, 1, 2))
    pair = zl // 2 * 2
    hzs = (zh, 1 - zh)

    count = [0]

    def sems(n):
        count[0] += n
        return count[0] - n

    r_g, r_b, r_zh = sems(6), sems(2 * NL), sems(1)
    r_y, r_c, r_co = sems(16), sems(16), sems(2)
    r_t, r_x, r_f = sems(2 * NL), sems(4 * NL), sems(2 * NL)
    r_w, r_v = sems(4), sems(NL)

    def copy(src, dst, s, r, dev):
        return pltpu.make_async_remote_copy(
            src_ref=src, dst_ref=dst, send_sem=send_sem.at[s], recv_sem=recv_sem.at[r],
            device_id=dev, device_id_type=MESH)

    def arrived(dst, r):
        copy(dst, dst, 0, r, xp).wait_recv()

    partners = (xp, xm, zp, zm, yp, ym, co)
    barrier = pltpu.get_barrier_semaphore()
    for dev in partners:
        pl.semaphore_signal(barrier, inc=1, device_id=dev, device_id_type=MESH)

    x_own = xbuf.at[ys[0], zh, c]
    load = [
        pltpu.make_async_copy(own_ref.at[pl.ds(0, 128)], gbuf.at[g_own], own_sem.at[0]),
        pltpu.make_async_copy(own_ref.at[pl.ds(128, 64)], bbuf.at[zl], own_sem.at[1]),
        pltpu.make_async_copy(
            own_ref.at[pl.ds(192, 48), pl.ds(0, 512)], x_own.at[pl.ds(0, 48)], own_sem.at[2]),
        pltpu.make_async_copy(
            own_ref.at[pl.ds(192, 32), pl.ds(512, 512)], x_own.at[pl.ds(48, 32)], own_sem.at[3]),
    ]
    for cp in load:
        cp.start()
    for cp in load:
        cp.wait()
    pl.semaphore_wait(barrier, len(partners))

    def tell(k):
        pl.semaphore_signal(level.at[k - 1], inc=1, device_id=zm, device_id_type=MESH)

    tell(1)

    def rot_x(t, _):
        data = xbuf[pl.ds(t * 2, 2), :, :, pl.ds(0, 64), :].reshape(512, 512)
        turned = dot_nt(bx[...], data).astype(jnp.bfloat16)
        rx[t] = turned
        sx[t] = square(turned)
        return 0

    def columns(dx, blocks, begin=True, end=True):
        cols = [
            pl.ds(pl.multiple_of((x + dx) % NX * 256 + p * 128, 128), 128)
            for p in (zl // 2, 1 - zl // 2)]

        def rows(m, _):
            here = pl.ds(pl.multiple_of(m * 256, 256), 256)
            if begin:
                grad = jnp.zeros((256, 256), jnp.float32)
                scale = jnp.zeros((256, 256), jnp.float32)
            else:
                grad, scale = acc[0, here, :], acc[1, here, :]
            for i in blocks:
                t = slots[i]
                halves = [rt[dx, t, A_ROWS, :], rt[dx, t, B_ROWS, :]]
                piece = jnp.concatenate(halves if i < 2 else halves[::-1], axis=0)
                grad += dot_nt(rx[t, here, :], piece)
                scale += dot_nt(sx[t, here, :], square(piece))
            if end:
                result = (grad / TOKENS) / (scale / TOKENS + DAMPING)
                out[here, cols[0]] = result[:, :128]
                out[here, cols[1]] = result[:, 128:]
            else:
                acc[0, here, :] = grad
                acc[1, here, :] = scale
            return 0

        lax.fori_loop(0, 2, rows, 0)

    def program(inside, order, finish):
        count = [0]

        def send(src, dst, r, dev):
            cp = copy(src, dst, count[0], r, dev)
            count[0] += 1
            if finish:
                cp.wait_send()
            else:
                cp.start()

        def recv(dst, r):
            if not finish:
                arrived(dst, r)

        def pass_on(ref, r, dev):
            send(ref, ref, r, dev)

        def own_z(ref, r):
            pass_on(ref, r, nb1)
            if inside:
                pass_on(ref, r, nb2)

        def next_z(e, ref, r):
            if inside:
                pass_on(ref, r, nb2 if e == 0 else nb1)

        def b_part(s, q):
            return bbuf.at[s, :, pl.ds(q * 512, 512)]

        def x_sends(i, h):
            s, r = slots[i], r_x + 4 * i + 2 * h
            rows = BZ_ROWS if h else A_ROWS
            send(rt.at[0, s, rows], rt.at[3, s, rows], r, xp)
            send(rt.at[0, s, rows], rt.at[1, s, rows], r + 1, xm)

        def tile(h):
            first = pair if h == 0 else 2 - pair
            rows = B_ROWS if h else A_ROWS
            if not finish:
                basis = bbuf[pl.ds(first, 2)].reshape(128, 1024)
                turned = dot_nt(basis, gbuf[...].reshape(512, 1024))
                rt[0, zl, rows, :] = turned.astype(jnp.bfloat16)
            own_z(rt.at[0, zl, rows], r_t + 2 * zl + h)
            x_sends(0, h)

        def y_event(flow, k):
            for way in range(2):
                src = xbuf.at[ys[(8 - k) % 8 if way == 0 else k], hzs[flow], c]
                to = yp if way == 0 else ym
                half = src.at[pl.ds(0, XROWS), LEFT if way == 0 else RIGHT]
                if k == 4:
                    src = half
                r = (flow * 4 + k - 1) * 2 + way
                recv(src, r_y + r)
                if k < 3:
                    pass_on(src, r_y + r + 2, to)
                elif k == 3:
                    pass_on(half, r_y + r + 2, to)
                pass_on(src, r_c + r, co)

        def event(name):
            kind = name[0]
            if kind == "L":
                if not finish:
                    pl.semaphore_wait(level.at[int(name[1]) - 1], 1)
                    if name != "L3":
                        tell(int(name[1]) + 1)
            elif name == "Z4":
                pass_on(x_own, r_zh, z4)
            elif name == "XZ":
                far = xbuf.at[ys[0], 1 - zh, c]
                recv(far, r_zh)
                pass_on(far, r_y + 8, yp)
                pass_on(far, r_y + 9, ym)
                pass_on(far, r_co + 1, co)
            elif kind == "Y":
                y_event(int(name[1]), int(name[2]))
            elif kind == "B":
                e = int(name[1])
                s = arrivals[e]
                for q in range(2):
                    recv(b_part(s, q), r_b + 2 * s + q)
                    next_z(e, b_part(s, q), r_b + 2 * s + q)
            elif name == "G1":
                recv(gbuf.at[g_m, h0], r_g)
                pass_on(gbuf.at[g_m, h0], r_g + 4, xp)
            elif name == "G2":
                recv(gbuf.at[g_p, h1], r_g + 1)
                pass_on(gbuf.at[g_p, h1], r_g + 5, xm)
            elif name == "GA":
                recv(gbuf.at[g_m, h1], r_g + 2)
                recv(gbuf.at[g_p, h0], r_g + 3)
                recv(gbuf.at[g_2, h0], r_g + 4)
                recv(gbuf.at[g_2, h1], r_g + 5)
                tile(0)
            elif name == "GB":
                tile(1)
            elif name == "WX":
                send(rt.at[0, zl, W_ROWS], rt.at[3, zl, W_ROWS], r_w, xp)
                send(rt.at[0, zl, W_ROWS], rt.at[1, zl, W_ROWS], r_w + 1, xm)
            elif name == "WF":
                recv(rt.at[3, zl, W_ROWS], r_w)
                send(rt.at[3, zl, W_ROWS, LEFT], rt.at[2, zl, W_ROWS, LEFT], r_w + 2, xp)
                recv(rt.at[1, zl, W_ROWS], r_w + 1)
                send(rt.at[1, zl, W_ROWS, RIGHT], rt.at[2, zl, W_ROWS, RIGHT], r_w + 3, xm)
            elif name == "WZ":
                recv(rt.at[2, zl, W_ROWS, LEFT], r_w + 2)
                recv(rt.at[2, zl, W_ROWS, RIGHT], r_w + 3)
                own_z(rt.at[pl.ds(1, 3), zl, W_ROWS], r_v + zl)
            elif kind == "V":
                e = int(name[1])
                s = arrivals[e]
                part = rt.at[pl.ds(1, 3), s, W_ROWS]
                recv(part, r_v + s)
                next_z(e, part, r_v + s)
            elif kind == "T":
                e, h = int(name[1]), "AB".index(name[2])
                s = arrivals[e]
                part = rt.at[0, s, B_ROWS if h else A_ROWS]
                recv(part, r_t + 2 * s + h)
                next_z(e, part, r_t + 2 * s + h)
                x_sends(e + 1, h)
            elif kind == "F":
                i, h = int(name[1]), "AB".index(name[2])
                s, rows, r = slots[i], BZ_ROWS if h else A_ROWS, r_x + 4 * i + 2 * h
                if along_plus(i, h):
                    recv(rt.at[3, s, rows], r)
                    send(rt.at[3, s, rows], rt.at[2, s, rows], r_f + 2 * i + h, xp)
                else:
                    recv(rt.at[1, s, rows], r + 1)
                    send(rt.at[1, s, rows], rt.at[2, s, rows], r_f + 2 * i + h, xm)
            elif finish:
                pass
            elif name == "RX":
                for flow in range(2):
                    recv(xbuf.at[ys[0], hzs[flow], 1 - c], r_co + flow)
                    for k in range(1, 5):
                        for way in range(2):
                            dst = xbuf.at[ys[(8 - k) % 8 if way == 0 else k], hzs[flow], 1 - c]
                            if k == 4:
                                dst = dst.at[pl.ds(0, XROWS), LEFT if way == 0 else RIGHT]
                            recv(dst, r_c + (flow * 4 + k - 1) * 2 + way)
                for i in range(32):
                    ih, iy, ic = i // 16, i // 2 % 8, i % 2
                    bx[pl.ds(i * 16, 16), :] = xbuf[iy % 4 * 2 + iy // 4, ih, ic, pl.ds(64, 16), :]
                lax.fori_loop(0, NL, rot_x, 0)
            elif name == "C0":
                columns(0, range(NL))

        h0, h1 = pl.ds(0, 64), pl.ds(64, 64)
        pass_on(gbuf.at[g_own, h0], r_g, xp)
        pass_on(gbuf.at[g_own, h1], r_g + 1, xm)
        for q in range(2):
            own_z(b_part(zl, q), r_b + 2 * zl + q)
        pass_on(x_own, r_y, yp)
        pass_on(x_own, r_y + 1, ym)
        pass_on(x_own, r_co, co)
        pass_on(gbuf.at[g_own, h1], r_g + 2, xp)
        pass_on(gbuf.at[g_own, h0], r_g + 3, xm)
        for name in order:
            event(name)

    def both(finish):
        pl.when(inner == 0)(lambda: program(False, END_ORDER, finish))
        pl.when(inner == 1)(lambda: program(True, INNER_ORDER, finish))

    both(False)
    for i in range(NL):
        for h in range(2):
            if along_plus(i, h):
                arrived(rt.at[1, slots[i], BZ_ROWS if h else A_ROWS], r_x + 4 * i + 2 * h + 1)
    columns(1, range(NL))
    for i in range(NL):
        for h in range(2):
            if not along_plus(i, h):
                arrived(rt.at[3, slots[i], BZ_ROWS if h else A_ROWS], r_x + 4 * i + 2 * h)
    columns(3, range(NL))
    for blocks in ((0, 1, 2), (3,)):
        for i in blocks:
            for h in range(2):
                arrived(rt.at[2, slots[i], BZ_ROWS if h else A_ROWS], r_f + 2 * i + h)
        columns(2, blocks, begin=0 in blocks, end=3 in blocks)
    both(True)


def per_device(activations, out_grads, in_basis, out_basis):
    bf = jnp.bfloat16
    vmem = pl.BlockSpec(memory_space=pltpu.VMEM)
    right = jnp.concatenate([activations[48:], in_basis.T, jnp.zeros((16, 512), bf)], axis=0)
    wide = jnp.concatenate([activations[:48], right], axis=1)
    own = jnp.concatenate([out_grads, out_basis.T, wide], axis=0)
    return pl.pallas_call(
        kernel,
        out_shape=jax.ShapeDtypeStruct((512, 1024), jnp.float32),
        in_specs=[vmem],
        out_specs=vmem,
        scratch_shapes=[
            pltpu.VMEM((NY, NH, 2, XROWS, 512), bf),
            pltpu.VMEM((NX, 128, 1024), bf),
            pltpu.VMEM((NL, 64, 1024), bf),
            pltpu.VMEM((NX, NL, 256, 512), bf),
            pltpu.VMEM((512, 512), bf),
            pltpu.VMEM((NL, 512, 512), bf),
            pltpu.VMEM((NL, 512, 512), bf),
            pltpu.VMEM((2, 512, 256), jnp.float32),
            pltpu.SemaphoreType.DMA((110,)),
            pltpu.SemaphoreType.DMA((100,)),
            pltpu.SemaphoreType.DMA((4,)),
            pltpu.SemaphoreType.REGULAR((3,)),
        ],
        compiler_params=pltpu.CompilerParams(
            collective_id=0, has_side_effects=True, vmem_limit_bytes=48 * 2**20),
        cost_estimate=pl.CostEstimate(
            flops=6 * 10**9, bytes_accessed=4 * 2**20, transcendentals=0),
        name="gather_and_scale",
    )(own)


def solution(mesh):
    in_specs = (P("fsdp", "rep"), P("rep", "fsdp"), P("rep", "fsdp"), P("fsdp", "rep"))
    out_specs = P("rep", "fsdp")
    return jax.shard_map(
        per_device, mesh=mesh, in_specs=in_specs, out_specs=out_specs, check_vma=False
    )
```

```python
import functools

import jax
import jax.numpy as jnp
from jax import lax
from jax.experimental import pallas as pl
from jax.experimental.pallas import tpu as pltpu
from jax.sharding import PartitionSpec as P

MESH = pl.DeviceIdType.MESH
DAMPING = 0.001
TOKENS = 2048
NX, NL, NH, NY = 4, 4, 2, 8
XROWS = 80
WROWS = 48
A_ROWS = pl.ds(0, 128)
B_ROWS = pl.ds(128, 128)
BZ_ROWS = pl.ds(128, 128 - WROWS)
W_ROWS = pl.ds(256 - WROWS, WROWS)
LEFT, RIGHT = pl.ds(0, 256), pl.ds(256, 256)
NT = (((1,), (1,)), ((), ()))
END_ORDER = (
    "L1", "L2", "Y01", "G1", "G2", "L3", "Z4", "B0", "B1", "Y02", "GA", "Y03", "B2", "GB", "XZ",
    "WX", "T0A", "Y11", "WF", "T0B", "T1A", "WZ", "Y12", "T1B", "F0A", "F0B", "T2A", "F1B",
    "Y13", "F1A", "Y04", "Y14", "T2B", "F2A", "F3A", "RX", "F2B", "V1", "V0", "F3B", "C0", "V2",
)
INNER_ORDER = (
    "L1", "L2", "B1", "B0", "G2", "L3", "G1", "Z4", "Y01", "B2", "GA", "Y02", "GB", "XZ", "WX",
    "Y03", "T0A", "T1A", "Y11", "WF", "T1B", "T0B", "F0A", "T2A", "Y12", "WZ", "Y13", "Y04",
    "T2B", "F2A", "F2B", "V0", "Y14", "F0B", "F1A", "F1B", "V1", "F3A", "V2", "RX", "F3B", "C0",
)


def dot_nt(a, b):
    return lax.dot_general(a, b, NT, preferred_element_type=jnp.float32)


def square(a):
    wide = a.astype(jnp.float32)
    return (wide * wide).astype(jnp.bfloat16)


def slot_of(x):
    return (x % 2) * 2 + x // 2


def along_plus(i, h):
    return (h + i) % 2 == 0


def kernel(own_ref, out, xbuf, gbuf, bbuf, rt, bx, rx, sx, acc, send_sem, recv_sem, own_sem, level):
    rep, f = lax.axis_index("rep"), lax.axis_index("fsdp")
    x, zl = rep // NL, rep % NL
    zh, y, c = f // 16, (f // 2) % NY, f % 2
    inner = (zl + 1) // 2 % 2
    xp = (((x + 1) % NX) * NL + zl, f)
    xm = (((x + 3) % NX) * NL + zl, f)
    arrivals = (zl + 1 - 2 * (zl % 2), 2 - zl // 2, 3 - 3 * (zl // 2))
    slots = (zl,) + arrivals
    nb1 = (x * NL + arrivals[0], f)
    nb2 = (x * NL + (3 - zl), f)
    z = zh * NL + zl
    zp, zm = (
        (x * NL + (z + d) % 8 % NL, (z + d) % 8 // NL * 16 + y * 2 + c) for d in (1, 7))
    yp = (rep, zh * 16 + ((y + 1) % NY) * 2 + c)
    ym = (rep, zh * 16 + ((y + 7) % NY) * 2 + c)
    z4 = (rep, (1 - zh) * 16 + y * 2 + c)
    co = (rep, f + 1 - 2 * c)
    ys = [((y + d) % NY) % 4 * 2 + ((y + d) % NY) // 4 for d in range(NY)]
    g_own, g_m, g_p, g_2 = (slot_of((x + d) % NX) for d in (0, 3, 1, 2))
    pair = zl // 2 * 2
    hzs = (zh, 1 - zh)

    count = [0]

    def sems(n):
        count[0] += n
        return count[0] - n

    r_g, r_b, r_zh = sems(6), sems(2 * NL), sems(1)
    r_y, r_c, r_co = sems(16), sems(16), sems(2)
    r_t, r_x, r_f = sems(2 * NL), sems(4 * NL), sems(2 * NL)
    r_w, r_v = sems(4), sems(NL)

    def copy(src, dst, s, r, dev):
        return pltpu.make_async_remote_copy(
            src_ref=src, dst_ref=dst, send_sem=send_sem.at[s], recv_sem=recv_sem.at[r],
            device_id=dev, device_id_type=MESH)

    def arrived(dst, r):
        copy(dst, dst, 0, r, xp).wait_recv()

    partners = (xp, xm, zp, zm, yp, ym, co)
    barrier = pltpu.get_barrier_semaphore()
    for dev in partners:
        pl.semaphore_signal(barrier, inc=1, device_id=dev, device_id_type=MESH)

    x_own = xbuf.at[ys[0], zh, c]
    load = [
        pltpu.make_async_copy(own_ref.at[pl.ds(0, 128)], gbuf.at[g_own], own_sem.at[0]),
        pltpu.make_async_copy(own_ref.at[pl.ds(128, 64)], bbuf.at[zl], own_sem.at[1]),
        pltpu.make_async_copy(own_ref.at[pl.ds(192, XROWS), pl.ds(0, 512)], x_own, own_sem.at[2]),
    ]
    for cp in load:
        cp.start()
    for cp in load:
        cp.wait()
    pl.semaphore_wait(barrier, len(partners))

    def tell(k):
        pl.semaphore_signal(level.at[k - 1], inc=1, device_id=zm, device_id_type=MESH)

    tell(1)

    def rot_x(t, _):
        data = xbuf[pl.ds(t * 2, 2), :, :, pl.ds(0, 64), :].reshape(512, 512)
        turned = dot_nt(bx[...], data).astype(jnp.bfloat16)
        rx[t] = turned
        sx[t] = square(turned)
        return 0

    def columns(dx, blocks, begin=True, end=True):
        cols = [
            pl.ds(pl.multiple_of((x + dx) % NX * 256 + p * 128, 128), 128)
            for p in (zl // 2, 1 - zl // 2)]

        def rows(m, _):
            here = pl.ds(pl.multiple_of(m * 256, 256), 256)
            if begin:
                grad = jnp.zeros((256, 256), jnp.float32)
                scale = jnp.zeros((256, 256), jnp.float32)
            else:
                grad, scale = acc[0, here, :], acc[1, here, :]
            for i in blocks:
                t = slots[i]
                halves = [rt[dx, t, A_ROWS, :], rt[dx, t, B_ROWS, :]]
                piece = jnp.concatenate(halves if i < 2 else halves[::-1], axis=0)
                grad += dot_nt(rx[t, here, :], piece)
                scale += dot_nt(sx[t, here, :], square(piece))
            if end:
                result = (grad / TOKENS) / (scale / TOKENS + DAMPING)
                out[here, cols[0]] = result[:, :128]
                out[here, cols[1]] = result[:, 128:]
            else:
                acc[0, here, :] = grad
                acc[1, here, :] = scale
            return 0

        lax.fori_loop(0, 2, rows, 0)

    def program(inside, order, finish):
        count = [0]

        def send(src, dst, r, dev):
            cp = copy(src, dst, count[0], r, dev)
            count[0] += 1
            if finish:
                cp.wait_send()
            else:
                cp.start()

        def recv(dst, r):
            if not finish:
                arrived(dst, r)

        def pass_on(ref, r, dev):
            send(ref, ref, r, dev)

        def own_z(ref, r):
            pass_on(ref, r, nb1)
            if inside:
                pass_on(ref, r, nb2)

        def next_z(e, ref, r):
            if inside:
                pass_on(ref, r, nb2 if e == 0 else nb1)

        def b_part(s, q):
            return bbuf.at[s, :, pl.ds(q * 512, 512)]

        def x_sends(i, h):
            s, r = slots[i], r_x + 4 * i + 2 * h
            rows = BZ_ROWS if h else A_ROWS
            send(rt.at[0, s, rows], rt.at[3, s, rows], r, xp)
            send(rt.at[0, s, rows], rt.at[1, s, rows], r + 1, xm)

        def tile(h):
            first = pair if h == 0 else 2 - pair
            rows = B_ROWS if h else A_ROWS
            if not finish:
                basis = bbuf[pl.ds(first, 2)].reshape(128, 1024)
                turned = dot_nt(basis, gbuf[...].reshape(512, 1024))
                rt[0, zl, rows, :] = turned.astype(jnp.bfloat16)
            own_z(rt.at[0, zl, rows], r_t + 2 * zl + h)
            x_sends(0, h)

        def y_event(flow, k):
            for way in range(2):
                src = xbuf.at[ys[(8 - k) % 8 if way == 0 else k], hzs[flow], c]
                to = yp if way == 0 else ym
                half = src.at[pl.ds(0, XROWS), LEFT if way == 0 else RIGHT]
                if k == 4:
                    src = half
                r = (flow * 4 + k - 1) * 2 + way
                recv(src, r_y + r)
                if k < 3:
                    pass_on(src, r_y + r + 2, to)
                elif k == 3:
                    pass_on(half, r_y + r + 2, to)
                pass_on(src, r_c + r, co)

        def event(name):
            kind = name[0]
            if kind == "L":
                if not finish:
                    pl.semaphore_wait(level.at[int(name[1]) - 1], 1)
                    if name != "L3":
                        tell(int(name[1]) + 1)
            elif name == "Z4":
                pass_on(x_own, r_zh, z4)
            elif name == "XZ":
                far = xbuf.at[ys[0], 1 - zh, c]
                recv(far, r_zh)
                pass_on(far, r_y + 8, yp)
                pass_on(far, r_y + 9, ym)
                pass_on(far, r_co + 1, co)
            elif kind == "Y":
                y_event(int(name[1]), int(name[2]))
            elif kind == "B":
                e = int(name[1])
                s = arrivals[e]
                for q in range(2):
                    recv(b_part(s, q), r_b + 2 * s + q)
                    next_z(e, b_part(s, q), r_b + 2 * s + q)
            elif name == "G1":
                recv(gbuf.at[g_m, h0], r_g)
                pass_on(gbuf.at[g_m, h0], r_g + 4, xp)
            elif name == "G2":
                recv(gbuf.at[g_p, h1], r_g + 1)
                pass_on(gbuf.at[g_p, h1], r_g + 5, xm)
            elif name == "GA":
                recv(gbuf.at[g_m, h1], r_g + 2)
                recv(gbuf.at[g_p, h0], r_g + 3)
                recv(gbuf.at[g_2, h0], r_g + 4)
                recv(gbuf.at[g_2, h1], r_g + 5)
                tile(0)
            elif name == "GB":
                tile(1)
            elif name == "WX":
                send(rt.at[0, zl, W_ROWS], rt.at[3, zl, W_ROWS], r_w, xp)
                send(rt.at[0, zl, W_ROWS], rt.at[1, zl, W_ROWS], r_w + 1, xm)
            elif name == "WF":
                recv(rt.at[3, zl, W_ROWS], r_w)
                send(rt.at[3, zl, W_ROWS, LEFT], rt.at[2, zl, W_ROWS, LEFT], r_w + 2, xp)
                recv(rt.at[1, zl, W_ROWS], r_w + 1)
                send(rt.at[1, zl, W_ROWS, RIGHT], rt.at[2, zl, W_ROWS, RIGHT], r_w + 3, xm)
            elif name == "WZ":
                recv(rt.at[2, zl, W_ROWS, LEFT], r_w + 2)
                recv(rt.at[2, zl, W_ROWS, RIGHT], r_w + 3)
                own_z(rt.at[pl.ds(1, 3), zl, W_ROWS], r_v + zl)
            elif kind == "V":
                e = int(name[1])
                s = arrivals[e]
                part = rt.at[pl.ds(1, 3), s, W_ROWS]
                recv(part, r_v + s)
                next_z(e, part, r_v + s)
            elif kind == "T":
                e, h = int(name[1]), "AB".index(name[2])
                s = arrivals[e]
                part = rt.at[0, s, B_ROWS if h else A_ROWS]
                recv(part, r_t + 2 * s + h)
                next_z(e, part, r_t + 2 * s + h)
                x_sends(e + 1, h)
            elif kind == "F":
                i, h = int(name[1]), "AB".index(name[2])
                s, rows, r = slots[i], BZ_ROWS if h else A_ROWS, r_x + 4 * i + 2 * h
                if along_plus(i, h):
                    recv(rt.at[3, s, rows], r)
                    send(rt.at[3, s, rows], rt.at[2, s, rows], r_f + 2 * i + h, xp)
                else:
                    recv(rt.at[1, s, rows], r + 1)
                    send(rt.at[1, s, rows], rt.at[2, s, rows], r_f + 2 * i + h, xm)
            elif finish:
                pass
            elif name == "RX":
                for flow in range(2):
                    recv(xbuf.at[ys[0], hzs[flow], 1 - c], r_co + flow)
                    for k in range(1, 5):
                        for way in range(2):
                            dst = xbuf.at[ys[(8 - k) % 8 if way == 0 else k], hzs[flow], 1 - c]
                            if k == 4:
                                dst = dst.at[pl.ds(0, XROWS), LEFT if way == 0 else RIGHT]
                            recv(dst, r_c + (flow * 4 + k - 1) * 2 + way)
                for i in range(32):
                    ih, iy, ic = i // 16, i // 2 % 8, i % 2
                    bx[pl.ds(i * 16, 16), :] = xbuf[iy % 4 * 2 + iy // 4, ih, ic, pl.ds(64, 16), :]
                lax.fori_loop(0, NL, rot_x, 0)
            elif name == "C0":
                columns(0, range(NL))

        h0, h1 = pl.ds(0, 64), pl.ds(64, 64)
        pass_on(gbuf.at[g_own, h0], r_g, xp)
        pass_on(gbuf.at[g_own, h1], r_g + 1, xm)
        for q in range(2):
            own_z(b_part(zl, q), r_b + 2 * zl + q)
        pass_on(x_own, r_y, yp)
        pass_on(x_own, r_y + 1, ym)
        pass_on(x_own, r_co, co)
        pass_on(gbuf.at[g_own, h1], r_g + 2, xp)
        pass_on(gbuf.at[g_own, h0], r_g + 3, xm)
        for name in order:
            event(name)

    def both(finish):
        pl.when(inner == 0)(lambda: program(False, END_ORDER, finish))
        pl.when(inner == 1)(lambda: program(True, INNER_ORDER, finish))

    both(False)
    for i in range(NL):
        for h in range(2):
            if along_plus(i, h):
                arrived(rt.at[1, slots[i], BZ_ROWS if h else A_ROWS], r_x + 4 * i + 2 * h + 1)
    columns(1, range(NL))
    for i in range(NL):
        for h in range(2):
            if not along_plus(i, h):
                arrived(rt.at[3, slots[i], BZ_ROWS if h else A_ROWS], r_x + 4 * i + 2 * h)
    columns(3, range(NL))
    for blocks in ((0, 1, 2), (3,)):
        for i in blocks:
            for h in range(2):
                arrived(rt.at[2, slots[i], BZ_ROWS if h else A_ROWS], r_f + 2 * i + h)
        columns(2, blocks, begin=0 in blocks, end=3 in blocks)
    both(True)


def per_device(activations, out_grads, in_basis, out_basis):
    bf = jnp.bfloat16
    vmem = pl.BlockSpec(memory_space=pltpu.VMEM)
    pads = ((0, 0), (0, 512))
    own = jnp.concatenate(
        [out_grads, out_basis.T, jnp.pad(activations, pads), jnp.pad(in_basis.T, pads)], axis=0)
    return pl.pallas_call(
        kernel,
        out_shape=jax.ShapeDtypeStruct((512, 1024), jnp.float32),
        in_specs=[vmem],
        out_specs=vmem,
        scratch_shapes=[
            pltpu.VMEM((NY, NH, 2, XROWS, 512), bf),
            pltpu.VMEM((NX, 128, 1024), bf),
            pltpu.VMEM((NL, 64, 1024), bf),
            pltpu.VMEM((NX, NL, 256, 512), bf),
            pltpu.VMEM((512, 512), bf),
            pltpu.VMEM((NL, 512, 512), bf),
            pltpu.VMEM((NL, 512, 512), bf),
            pltpu.VMEM((2, 512, 256), jnp.float32),
            pltpu.SemaphoreType.DMA((110,)),
            pltpu.SemaphoreType.DMA((100,)),
            pltpu.SemaphoreType.DMA((3,)),
            pltpu.SemaphoreType.REGULAR((3,)),
        ],
        compiler_params=pltpu.CompilerParams(
            collective_id=0, has_side_effects=True, vmem_limit_bytes=48 * 2**20),
        cost_estimate=pl.CostEstimate(
            flops=6 * 10**9, bytes_accessed=4 * 2**20, transcendentals=0),
        name="gather_and_scale",
    )(own)


def solution(mesh):
    in_specs = (P("fsdp", "rep"), P("rep", "fsdp"), P("rep", "fsdp"), P("fsdp", "rep"))
    out_specs = P("rep", "fsdp")
    return jax.shard_map(
        per_device, mesh=mesh, in_specs=in_specs, out_specs=out_specs, check_vma=False
    )
```

```python
import functools

import jax
import jax.numpy as jnp
from jax import lax
from jax.experimental import pallas as pl
from jax.experimental.pallas import tpu as pltpu
from jax.sharding import PartitionSpec as P

MESH = pl.DeviceIdType.MESH
DAMPING = 0.001
TOKENS = 2048
NX, NL, NH, NY = 4, 4, 2, 8
XROWS = 80
WROWS = 48
A_ROWS = pl.ds(0, 128)
B_ROWS = pl.ds(128, 128)
BZ_ROWS = pl.ds(128, 128 - WROWS)
W_ROWS = pl.ds(256 - WROWS, WROWS)
LEFT, RIGHT = pl.ds(0, 256), pl.ds(256, 256)
NT = (((1,), (1,)), ((), ()))
END_ORDER = (
    "L1", "L2", "Y01", "G1", "G2", "L3", "Z4", "B0", "B1", "Y02", "GA", "Y03", "B2", "GB", "XZ",
    "WX", "T0A", "Y11", "WF", "T0B", "T1A", "WZ", "Y12", "T1B", "F0A", "F0B", "T2A", "F1B",
    "Y13", "F1A", "Y04", "Y14", "T2B", "F2A", "F3A", "RX", "F2B", "V1", "V0", "F3B",  "V2",
)
INNER_ORDER = (
    "L1", "L2", "B1", "B0", "G2", "L3", "G1", "Z4", "Y01", "B2", "GA", "Y02", "GB", "XZ", "WX",
    "Y03", "T0A", "T1A", "Y11", "WF", "T1B", "T0B", "F0A", "T2A", "Y12", "WZ", "Y13", "Y04",
    "T2B", "F2A", "F2B", "V0", "Y14", "F0B", "F1A", "F1B", "V1", "F3A", "V2", "RX", "F3B",
)


def dot_nt(a, b):
    return lax.dot_general(a, b, NT, preferred_element_type=jnp.float32)


def square(a):
    wide = a.astype(jnp.float32)
    return (wide * wide).astype(jnp.bfloat16)


def slot_of(x):
    return (x % 2) * 2 + x // 2


def along_plus(i, h):
    return (h + i) % 2 == 0


def kernel(own_ref, out, xbuf, gbuf, bbuf, rt, bx, rx, sx, acc, send_sem, recv_sem, own_sem, level):
    rep, f = lax.axis_index("rep"), lax.axis_index("fsdp")
    x, zl = rep // NL, rep % NL
    zh, y, c = f // 16, (f // 2) % NY, f % 2
    inner = (zl + 1) // 2 % 2
    xp = (((x + 1) % NX) * NL + zl, f)
    xm = (((x + 3) % NX) * NL + zl, f)
    arrivals = (zl + 1 - 2 * (zl % 2), 2 - zl // 2, 3 - 3 * (zl // 2))
    slots = (zl,) + arrivals
    nb1 = (x * NL + arrivals[0], f)
    nb2 = (x * NL + (3 - zl), f)
    z = zh * NL + zl
    zp, zm = (
        (x * NL + (z + d) % 8 % NL, (z + d) % 8 // NL * 16 + y * 2 + c) for d in (1, 7))
    yp = (rep, zh * 16 + ((y + 1) % NY) * 2 + c)
    ym = (rep, zh * 16 + ((y + 7) % NY) * 2 + c)
    z4 = (rep, (1 - zh) * 16 + y * 2 + c)
    co = (rep, f + 1 - 2 * c)
    ys = [((y + d) % NY) % 4 * 2 + ((y + d) % NY) // 4 for d in range(NY)]
    g_own, g_m, g_p, g_2 = (slot_of((x + d) % NX) for d in (0, 3, 1, 2))
    pair = zl // 2 * 2
    hzs = (zh, 1 - zh)

    count = [0]

    def sems(n):
        count[0] += n
        return count[0] - n

    r_g, r_b, r_zh = sems(6), sems(2 * NL), sems(1)
    r_y, r_c, r_co = sems(16), sems(16), sems(2)
    r_t, r_x, r_f = sems(2 * NL), sems(4 * NL), sems(2 * NL)
    r_w, r_v = sems(4), sems(NL)

    def copy(src, dst, s, r, dev):
        return pltpu.make_async_remote_copy(
            src_ref=src, dst_ref=dst, send_sem=send_sem.at[s], recv_sem=recv_sem.at[r],
            device_id=dev, device_id_type=MESH)

    def arrived(dst, r):
        copy(dst, dst, 0, r, xp).wait_recv()

    partners = (xp, xm, zp, zm, yp, ym, co)
    barrier = pltpu.get_barrier_semaphore()
    for dev in partners:
        pl.semaphore_signal(barrier, inc=1, device_id=dev, device_id_type=MESH)

    x_own = xbuf.at[ys[0], zh, c]
    load = [
        pltpu.make_async_copy(own_ref.at[pl.ds(0, 128)], gbuf.at[g_own], own_sem.at[0]),
        pltpu.make_async_copy(own_ref.at[pl.ds(128, 64)], bbuf.at[zl], own_sem.at[1]),
        pltpu.make_async_copy(own_ref.at[pl.ds(192, XROWS), pl.ds(0, 512)], x_own, own_sem.at[2]),
    ]
    for cp in load:
        cp.start()
    for cp in load:
        cp.wait()
    pl.semaphore_wait(barrier, len(partners))

    def tell(k):
        pl.semaphore_signal(level.at[k - 1], inc=1, device_id=zm, device_id_type=MESH)

    tell(1)

    def rot_x(t, _):
        data = xbuf[pl.ds(t * 2, 2), :, :, pl.ds(0, 64), :].reshape(512, 512)
        turned = dot_nt(bx[...], data).astype(jnp.bfloat16)
        rx[t] = turned
        sx[t] = square(turned)
        return 0

    def columns(dx, blocks, begin=True, end=True):
        cols = [
            pl.ds(pl.multiple_of((x + dx) % NX * 256 + p * 128, 128), 128)
            for p in (zl // 2, 1 - zl // 2)]

        def rows(m, _):
            here = pl.ds(pl.multiple_of(m * 256, 256), 256)
            if begin:
                grad = jnp.zeros((256, 256), jnp.float32)
                scale = jnp.zeros((256, 256), jnp.float32)
            else:
                grad, scale = acc[0, here, :], acc[1, here, :]
            for i in blocks:
                t = slots[i]
                halves = [rt[dx, t, A_ROWS, :], rt[dx, t, B_ROWS, :]]
                piece = jnp.concatenate(halves if i < 2 else halves[::-1], axis=0)
                grad += dot_nt(rx[t, here, :], piece)
                scale += dot_nt(sx[t, here, :], square(piece))
            if end:
                result = (grad / TOKENS) / (scale / TOKENS + DAMPING)
                out[here, cols[0]] = result[:, :128]
                out[here, cols[1]] = result[:, 128:]
            else:
                acc[0, here, :] = grad
                acc[1, here, :] = scale
            return 0

        lax.fori_loop(0, 2, rows, 0)

    def program(inside, order, finish):
        count = [0]

        def send(src, dst, r, dev):
            cp = copy(src, dst, count[0], r, dev)
            count[0] += 1
            if finish:
                cp.wait_send()
            else:
                cp.start()

        def recv(dst, r):
            if not finish:
                arrived(dst, r)

        def pass_on(ref, r, dev):
            send(ref, ref, r, dev)

        def own_z(ref, r):
            pass_on(ref, r, nb1)
            if inside:
                pass_on(ref, r, nb2)

        def next_z(e, ref, r):
            if inside:
                pass_on(ref, r, nb2 if e == 0 else nb1)

        def b_part(s, q):
            return bbuf.at[s, :, pl.ds(q * 512, 512)]

        def x_sends(i, h):
            s, r = slots[i], r_x + 4 * i + 2 * h
            rows = BZ_ROWS if h else A_ROWS
            send(rt.at[0, s, rows], rt.at[3, s, rows], r, xp)
            send(rt.at[0, s, rows], rt.at[1, s, rows], r + 1, xm)

        def tile(h):
            first = pair if h == 0 else 2 - pair
            rows = B_ROWS if h else A_ROWS
            if not finish:
                basis = bbuf[pl.ds(first, 2)].reshape(128, 1024)
                turned = dot_nt(basis, gbuf[...].reshape(512, 1024))
                rt[0, zl, rows, :] = turned.astype(jnp.bfloat16)
            own_z(rt.at[0, zl, rows], r_t + 2 * zl + h)
            x_sends(0, h)

        def y_event(flow, k):
            for way in range(2):
                src = xbuf.at[ys[(8 - k) % 8 if way == 0 else k], hzs[flow], c]
                to = yp if way == 0 else ym
                half = src.at[pl.ds(0, XROWS), LEFT if way == 0 else RIGHT]
                if k == 4:
                    src = half
                r = (flow * 4 + k - 1) * 2 + way
                recv(src, r_y + r)
                if k < 3:
                    pass_on(src, r_y + r + 2, to)
                elif k == 3:
                    pass_on(half, r_y + r + 2, to)
                pass_on(src, r_c + r, co)

        def event(name):
            kind = name[0]
            if kind == "L":
                if not finish:
                    pl.semaphore_wait(level.at[int(name[1]) - 1], 1)
                    if name != "L3":
                        tell(int(name[1]) + 1)
            elif name == "Z4":
                pass_on(x_own, r_zh, z4)
            elif name == "XZ":
                far = xbuf.at[ys[0], 1 - zh, c]
                recv(far, r_zh)
                pass_on(far, r_y + 8, yp)
                pass_on(far, r_y + 9, ym)
                pass_on(far, r_co + 1, co)
            elif kind == "Y":
                y_event(int(name[1]), int(name[2]))
            elif kind == "B":
                e = int(name[1])
                s = arrivals[e]
                for q in range(2):
                    recv(b_part(s, q), r_b + 2 * s + q)
                    next_z(e, b_part(s, q), r_b + 2 * s + q)
            elif name == "G1":
                recv(gbuf.at[g_m, h0], r_g)
                pass_on(gbuf.at[g_m, h0], r_g + 4, xp)
            elif name == "G2":
                recv(gbuf.at[g_p, h1], r_g + 1)
                pass_on(gbuf.at[g_p, h1], r_g + 5, xm)
            elif name == "GA":
                recv(gbuf.at[g_m, h1], r_g + 2)
                recv(gbuf.at[g_p, h0], r_g + 3)
                recv(gbuf.at[g_2, h0], r_g + 4)
                recv(gbuf.at[g_2, h1], r_g + 5)
                tile(0)
            elif name == "GB":
                tile(1)
            elif name == "WX":
                send(rt.at[0, zl, W_ROWS], rt.at[3, zl, W_ROWS], r_w, xp)
                send(rt.at[0, zl, W_ROWS], rt.at[1, zl, W_ROWS], r_w + 1, xm)
            elif name == "WF":
                recv(rt.at[3, zl, W_ROWS], r_w)
                send(rt.at[3, zl, W_ROWS, LEFT], rt.at[2, zl, W_ROWS, LEFT], r_w + 2, xp)
                recv(rt.at[1, zl, W_ROWS], r_w + 1)
                send(rt.at[1, zl, W_ROWS, RIGHT], rt.at[2, zl, W_ROWS, RIGHT], r_w + 3, xm)
            elif name == "WZ":
                recv(rt.at[2, zl, W_ROWS, LEFT], r_w + 2)
                recv(rt.at[2, zl, W_ROWS, RIGHT], r_w + 3)
                own_z(rt.at[pl.ds(1, 3), zl, W_ROWS], r_v + zl)
            elif kind == "V":
                e = int(name[1])
                s = arrivals[e]
                part = rt.at[pl.ds(1, 3), s, W_ROWS]
                recv(part, r_v + s)
                next_z(e, part, r_v + s)
            elif kind == "T":
                e, h = int(name[1]), "AB".index(name[2])
                s = arrivals[e]
                part = rt.at[0, s, B_ROWS if h else A_ROWS]
                recv(part, r_t + 2 * s + h)
                next_z(e, part, r_t + 2 * s + h)
                x_sends(e + 1, h)
            elif kind == "F":
                i, h = int(name[1]), "AB".index(name[2])
                s, rows, r = slots[i], BZ_ROWS if h else A_ROWS, r_x + 4 * i + 2 * h
                if along_plus(i, h):
                    recv(rt.at[3, s, rows], r)
                    send(rt.at[3, s, rows], rt.at[2, s, rows], r_f + 2 * i + h, xp)
                else:
                    recv(rt.at[1, s, rows], r + 1)
                    send(rt.at[1, s, rows], rt.at[2, s, rows], r_f + 2 * i + h, xm)
            elif finish:
                pass
            elif name == "RX":
                for flow in range(2):
                    recv(xbuf.at[ys[0], hzs[flow], 1 - c], r_co + flow)
                    for k in range(1, 5):
                        for way in range(2):
                            dst = xbuf.at[ys[(8 - k) % 8 if way == 0 else k], hzs[flow], 1 - c]
                            if k == 4:
                                dst = dst.at[pl.ds(0, XROWS), LEFT if way == 0 else RIGHT]
                            recv(dst, r_c + (flow * 4 + k - 1) * 2 + way)
                for i in range(32):
                    ih, iy, ic = i // 16, i // 2 % 8, i % 2
                    bx[pl.ds(i * 16, 16), :] = xbuf[iy % 4 * 2 + iy // 4, ih, ic, pl.ds(64, 16), :]
                lax.fori_loop(0, NL, rot_x, 0)

        h0, h1 = pl.ds(0, 64), pl.ds(64, 64)
        pass_on(gbuf.at[g_own, h0], r_g, xp)
        pass_on(gbuf.at[g_own, h1], r_g + 1, xm)
        for q in range(2):
            own_z(b_part(zl, q), r_b + 2 * zl + q)
        pass_on(x_own, r_y, yp)
        pass_on(x_own, r_y + 1, ym)
        pass_on(x_own, r_co, co)
        pass_on(gbuf.at[g_own, h1], r_g + 2, xp)
        pass_on(gbuf.at[g_own, h0], r_g + 3, xm)
        for name in order:
            event(name)

    def both(finish):
        pl.when(inner == 0)(lambda: program(False, END_ORDER, finish))
        pl.when(inner == 1)(lambda: program(True, INNER_ORDER, finish))

    both(False)
    columns(0, range(NL))
    for i in range(NL):
        for h in range(2):
            if along_plus(i, h):
                arrived(rt.at[1, slots[i], BZ_ROWS if h else A_ROWS], r_x + 4 * i + 2 * h + 1)
    columns(1, range(NL))
    for i in range(NL):
        for h in range(2):
            if not along_plus(i, h):
                arrived(rt.at[3, slots[i], BZ_ROWS if h else A_ROWS], r_x + 4 * i + 2 * h)
    columns(3, range(NL))
    for blocks in ((0, 1, 2), (3,)):
        if 3 in blocks:
            both(True)
        for i in blocks:
            for h in range(2):
                arrived(rt.at[2, slots[i], BZ_ROWS if h else A_ROWS], r_f + 2 * i + h)
        columns(2, blocks, begin=0 in blocks, end=3 in blocks)


def per_device(activations, out_grads, in_basis, out_basis):
    bf = jnp.bfloat16
    vmem = pl.BlockSpec(memory_space=pltpu.VMEM)
    pads = ((0, 0), (0, 512))
    own = jnp.concatenate(
        [out_grads, out_basis.T, jnp.pad(activations, pads), jnp.pad(in_basis.T, pads)], axis=0)
    return pl.pallas_call(
        kernel,
        out_shape=jax.ShapeDtypeStruct((512, 1024), jnp.float32),
        in_specs=[vmem],
        out_specs=vmem,
        scratch_shapes=[
            pltpu.VMEM((NY, NH, 2, XROWS, 512), bf),
            pltpu.VMEM((NX, 128, 1024), bf),
            pltpu.VMEM((NL, 64, 1024), bf),
            pltpu.VMEM((NX, NL, 256, 512), bf),
            pltpu.VMEM((512, 512), bf),
            pltpu.VMEM((NL, 512, 512), bf),
            pltpu.VMEM((NL, 512, 512), bf),
            pltpu.VMEM((2, 512, 256), jnp.float32),
            pltpu.SemaphoreType.DMA((110,)),
            pltpu.SemaphoreType.DMA((100,)),
            pltpu.SemaphoreType.DMA((3,)),
            pltpu.SemaphoreType.REGULAR((3,)),
        ],
        compiler_params=pltpu.CompilerParams(
            collective_id=0, has_side_effects=True, vmem_limit_bytes=48 * 2**20),
        cost_estimate=pl.CostEstimate(
            flops=6 * 10**9, bytes_accessed=4 * 2**20, transcendentals=0),
        name="gather_and_scale",
    )(own)


def solution(mesh):
    in_specs = (P("fsdp", "rep"), P("rep", "fsdp"), P("rep", "fsdp"), P("fsdp", "rep"))
    out_specs = P("rep", "fsdp")
    return jax.shard_map(
        per_device, mesh=mesh, in_specs=in_specs, out_specs=out_specs, check_vma=False
    )
```

```python
import functools

import jax
import jax.numpy as jnp
from jax import lax
from jax.experimental import pallas as pl
from jax.experimental.pallas import tpu as pltpu
from jax.sharding import PartitionSpec as P

MESH = pl.DeviceIdType.MESH
DAMPING = 0.001
TOKENS = 2048
NX, NL, NH, NY = 4, 4, 2, 8
XROWS = 80
WROWS = 48
A_ROWS = pl.ds(0, 128)
B_ROWS = pl.ds(128, 128)
BZ_ROWS = pl.ds(128, 128 - WROWS)
W_ROWS = pl.ds(256 - WROWS, WROWS)
LEFT, RIGHT = pl.ds(0, 256), pl.ds(256, 256)
NT = (((1,), (1,)), ((), ()))
END_ORDER = (
    "G1", "Y01", "B0", "Z4", "G2", "Y02", "GA", "B1", "B2", "GB", "XZ", "Y03", "WX", "T0A",
    "Y11", "WF", "T0B", "F0A", "T1A", "Y04", "F0B", "WZ", "Y12", "T1B", "Y13", "T2A", "T2B",
    "F2A", "Y14", "F2B", "F1A", "V0", "F1B", "F3A", "RX", "F3B", "V1", "V2",
)
INNER_ORDER = (
    "Z4", "G1", "B0", "G2", "Y01", "B1", "B2", "GA", "Y02", "GB", "WX", "XZ", "T0A", "T1A",
    "Y03", "Y11", "WF", "T1B", "T0B", "Y04", "Y12", "T2A", "T2B", "WZ", "Y13", "F2A", "V0",
    "F1B", "Y14", "F0B", "F2B", "F0A", "F1A", "V1", "F3B", "V2", "RX", "F3A",
)


def dot_nt(a, b):
    return lax.dot_general(a, b, NT, preferred_element_type=jnp.float32)


def square(a):
    wide = a.astype(jnp.float32)
    return (wide * wide).astype(jnp.bfloat16)


def slot_of(x):
    return (x % 2) * 2 + x // 2


def along_plus(i, h):
    return (h + i) % 2 == 0


def kernel(own_ref, out, xbuf, gbuf, bbuf, rt, bx, rx, sx, acc, send_sem, recv_sem, own_sem):
    rep, f = lax.axis_index("rep"), lax.axis_index("fsdp")
    x, zl = rep // NL, rep % NL
    zh, y, c = f // 16, (f // 2) % NY, f % 2
    inner = (zl + 1) // 2 % 2
    xp = (((x + 1) % NX) * NL + zl, f)
    xm = (((x + 3) % NX) * NL + zl, f)
    arrivals = (zl + 1 - 2 * (zl % 2), 2 - zl // 2, 3 - 3 * (zl // 2))
    slots = (zl,) + arrivals
    nb1 = (x * NL + arrivals[0], f)
    nb2 = (x * NL + (3 - zl), f)
    z = zh * NL + zl
    zp, zm = (
        (x * NL + (z + d) % 8 % NL, (z + d) % 8 // NL * 16 + y * 2 + c) for d in (1, 7))
    yp = (rep, zh * 16 + ((y + 1) % NY) * 2 + c)
    ym = (rep, zh * 16 + ((y + 7) % NY) * 2 + c)
    z4 = (rep, (1 - zh) * 16 + y * 2 + c)
    co = (rep, f + 1 - 2 * c)
    ys = [((y + d) % NY) % 4 * 2 + ((y + d) % NY) // 4 for d in range(NY)]
    g_own, g_m, g_p, g_2 = (slot_of((x + d) % NX) for d in (0, 3, 1, 2))
    pair = zl // 2 * 2
    hzs = (zh, 1 - zh)

    count = [0]

    def sems(n):
        count[0] += n
        return count[0] - n

    r_g, r_b, r_zh = sems(6), sems(2 * NL), sems(1)
    r_y, r_c, r_co = sems(16), sems(16), sems(2)
    r_t, r_x, r_f = sems(2 * NL), sems(4 * NL), sems(2 * NL)
    r_w, r_v = sems(4), sems(NL)

    def copy(src, dst, s, r, dev):
        return pltpu.make_async_remote_copy(
            src_ref=src, dst_ref=dst, send_sem=send_sem.at[s], recv_sem=recv_sem.at[r],
            device_id=dev, device_id_type=MESH)

    def arrived(dst, r):
        copy(dst, dst, 0, r, xp).wait_recv()

    partners = (xp, xm, zp, zm, z4, yp, ym, co)
    barrier = pltpu.get_barrier_semaphore()
    for dev in partners:
        pl.semaphore_signal(barrier, inc=1, device_id=dev, device_id_type=MESH)

    x_own = xbuf.at[ys[0], zh, c]
    load = [
        pltpu.make_async_copy(own_ref.at[pl.ds(0, 128)], gbuf.at[g_own], own_sem.at[0]),
        pltpu.make_async_copy(own_ref.at[pl.ds(128, 64)], bbuf.at[zl], own_sem.at[1]),
        pltpu.make_async_copy(own_ref.at[pl.ds(192, XROWS), pl.ds(0, 512)], x_own, own_sem.at[2]),
    ]
    for cp in load:
        cp.start()
    for cp in load:
        cp.wait()
    pl.semaphore_wait(barrier, len(partners))

    def rot_x(t, _):
        data = xbuf[pl.ds(t * 2, 2), :, :, pl.ds(0, 64), :].reshape(512, 512)
        turned = dot_nt(bx[...], data).astype(jnp.bfloat16)
        rx[t] = turned
        sx[t] = square(turned)
        return 0

    def columns(dx, blocks, begin=True, end=True):
        cols = [
            pl.ds(pl.multiple_of((x + dx) % NX * 256 + p * 128, 128), 128)
            for p in (zl // 2, 1 - zl // 2)]

        def rows(m, _):
            here = pl.ds(pl.multiple_of(m * 256, 256), 256)
            if begin:
                grad = jnp.zeros((256, 256), jnp.float32)
                scale = jnp.zeros((256, 256), jnp.float32)
            else:
                grad, scale = acc[0, here, :], acc[1, here, :]
            for i in blocks:
                t = slots[i]
                halves = [rt[dx, t, A_ROWS, :], rt[dx, t, B_ROWS, :]]
                piece = jnp.concatenate(halves if i < 2 else halves[::-1], axis=0)
                grad += dot_nt(rx[t, here, :], piece)
                scale += dot_nt(sx[t, here, :], square(piece))
            if end:
                result = (grad / TOKENS) / (scale / TOKENS + DAMPING)
                out[here, cols[0]] = result[:, :128]
                out[here, cols[1]] = result[:, 128:]
            else:
                acc[0, here, :] = grad
                acc[1, here, :] = scale
            return 0

        lax.fori_loop(0, 2, rows, 0)

    def program(inside, order, finish):
        count = [0]

        def send(src, dst, r, dev):
            cp = copy(src, dst, count[0], r, dev)
            count[0] += 1
            if finish:
                cp.wait_send()
            else:
                cp.start()

        def recv(dst, r):
            if not finish:
                arrived(dst, r)

        def pass_on(ref, r, dev):
            send(ref, ref, r, dev)

        def own_z(ref, r):
            pass_on(ref, r, nb1)
            if inside:
                pass_on(ref, r, nb2)

        def next_z(e, ref, r):
            if inside:
                pass_on(ref, r, nb2 if e == 0 else nb1)

        def b_part(s, q):
            return bbuf.at[s, :, pl.ds(q * 512, 512)]

        def x_sends(i, h):
            s, r = slots[i], r_x + 4 * i + 2 * h
            rows = BZ_ROWS if h else A_ROWS
            send(rt.at[0, s, rows], rt.at[3, s, rows], r, xp)
            send(rt.at[0, s, rows], rt.at[1, s, rows], r + 1, xm)

        def tile(h):
            first = pair if h == 0 else 2 - pair
            rows = B_ROWS if h else A_ROWS
            if not finish:
                basis = bbuf[pl.ds(first, 2)].reshape(128, 1024)
                turned = dot_nt(basis, gbuf[...].reshape(512, 1024))
                rt[0, zl, rows, :] = turned.astype(jnp.bfloat16)
            own_z(rt.at[0, zl, rows], r_t + 2 * zl + h)
            x_sends(0, h)

        def y_event(flow, k):
            for way in range(2):
                src = xbuf.at[ys[(8 - k) % 8 if way == 0 else k], hzs[flow], c]
                to = yp if way == 0 else ym
                half = src.at[pl.ds(0, XROWS), LEFT if way == 0 else RIGHT]
                if k == 4:
                    src = half
                r = (flow * 4 + k - 1) * 2 + way
                recv(src, r_y + r)
                if k < 3:
                    pass_on(src, r_y + r + 2, to)
                elif k == 3:
                    pass_on(half, r_y + r + 2, to)
                pass_on(src, r_c + r, co)

        def event(name):
            kind = name[0]
            if name == "Z4":
                pass_on(x_own, r_zh, z4)
            elif name == "XZ":
                far = xbuf.at[ys[0], 1 - zh, c]
                recv(far, r_zh)
                pass_on(far, r_y + 8, yp)
                pass_on(far, r_y + 9, ym)
                pass_on(far, r_co + 1, co)
            elif kind == "Y":
                y_event(int(name[1]), int(name[2]))
            elif kind == "B":
                e = int(name[1])
                s = arrivals[e]
                for q in range(2):
                    recv(b_part(s, q), r_b + 2 * s + q)
                    next_z(e, b_part(s, q), r_b + 2 * s + q)
            elif name == "G1":
                recv(gbuf.at[g_m, h0], r_g)
                pass_on(gbuf.at[g_m, h0], r_g + 4, xp)
            elif name == "G2":
                recv(gbuf.at[g_p, h1], r_g + 1)
                pass_on(gbuf.at[g_p, h1], r_g + 5, xm)
            elif name == "GA":
                recv(gbuf.at[g_m, h1], r_g + 2)
                recv(gbuf.at[g_p, h0], r_g + 3)
                recv(gbuf.at[g_2, h0], r_g + 4)
                recv(gbuf.at[g_2, h1], r_g + 5)
                tile(0)
            elif name == "GB":
                tile(1)
            elif name == "WX":
                send(rt.at[0, zl, W_ROWS], rt.at[3, zl, W_ROWS], r_w, xp)
                send(rt.at[0, zl, W_ROWS], rt.at[1, zl, W_ROWS], r_w + 1, xm)
            elif name == "WF":
                recv(rt.at[3, zl, W_ROWS], r_w)
                send(rt.at[3, zl, W_ROWS, LEFT], rt.at[2, zl, W_ROWS, LEFT], r_w + 2, xp)
                recv(rt.at[1, zl, W_ROWS], r_w + 1)
                send(rt.at[1, zl, W_ROWS, RIGHT], rt.at[2, zl, W_ROWS, RIGHT], r_w + 3, xm)
            elif name == "WZ":
                recv(rt.at[2, zl, W_ROWS, LEFT], r_w + 2)
                recv(rt.at[2, zl, W_ROWS, RIGHT], r_w + 3)
                own_z(rt.at[pl.ds(1, 3), zl, W_ROWS], r_v + zl)
            elif kind == "V":
                e = int(name[1])
                s = arrivals[e]
                part = rt.at[pl.ds(1, 3), s, W_ROWS]
                recv(part, r_v + s)
                next_z(e, part, r_v + s)
            elif kind == "T":
                e, h = int(name[1]), "AB".index(name[2])
                s = arrivals[e]
                part = rt.at[0, s, B_ROWS if h else A_ROWS]
                recv(part, r_t + 2 * s + h)
                next_z(e, part, r_t + 2 * s + h)
                x_sends(e + 1, h)
            elif kind == "F":
                i, h = int(name[1]), "AB".index(name[2])
                s, rows, r = slots[i], BZ_ROWS if h else A_ROWS, r_x + 4 * i + 2 * h
                if along_plus(i, h):
                    recv(rt.at[3, s, rows], r)
                    send(rt.at[3, s, rows], rt.at[2, s, rows], r_f + 2 * i + h, xp)
                else:
                    recv(rt.at[1, s, rows], r + 1)
                    send(rt.at[1, s, rows], rt.at[2, s, rows], r_f + 2 * i + h, xm)
            elif finish:
                pass
            elif name == "RX":
                for flow in range(2):
                    recv(xbuf.at[ys[0], hzs[flow], 1 - c], r_co + flow)
                    for k in range(1, 5):
                        for way in range(2):
                            dst = xbuf.at[ys[(8 - k) % 8 if way == 0 else k], hzs[flow], 1 - c]
                            if k == 4:
                                dst = dst.at[pl.ds(0, XROWS), LEFT if way == 0 else RIGHT]
                            recv(dst, r_c + (flow * 4 + k - 1) * 2 + way)
                for i in range(32):
                    ih, iy, ic = i // 16, i // 2 % 8, i % 2
                    bx[pl.ds(i * 16, 16), :] = xbuf[iy % 4 * 2 + iy // 4, ih, ic, pl.ds(64, 16), :]
                lax.fori_loop(0, NL, rot_x, 0)

        h0, h1 = pl.ds(0, 64), pl.ds(64, 64)
        pass_on(gbuf.at[g_own, h0], r_g, xp)
        pass_on(gbuf.at[g_own, h1], r_g + 1, xm)
        for q in range(2):
            own_z(b_part(zl, q), r_b + 2 * zl + q)
        pass_on(x_own, r_y, yp)
        pass_on(x_own, r_y + 1, ym)
        pass_on(x_own, r_co, co)
        pass_on(gbuf.at[g_own, h1], r_g + 2, xp)
        pass_on(gbuf.at[g_own, h0], r_g + 3, xm)
        for name in order:
            event(name)

    def both(finish):
        pl.when(inner == 0)(lambda: program(False, END_ORDER, finish))
        pl.when(inner == 1)(lambda: program(True, INNER_ORDER, finish))

    both(False)
    columns(0, range(NL))
    for i in range(NL):
        for h in range(2):
            if along_plus(i, h):
                arrived(rt.at[1, slots[i], BZ_ROWS if h else A_ROWS], r_x + 4 * i + 2 * h + 1)
    columns(1, range(NL))
    for i in range(NL):
        for h in range(2):
            if not along_plus(i, h):
                arrived(rt.at[3, slots[i], BZ_ROWS if h else A_ROWS], r_x + 4 * i + 2 * h)
    columns(3, range(NL))
    for blocks in ((0, 1, 2), (3,)):
        if 3 in blocks:
            both(True)
        for i in blocks:
            for h in range(2):
                arrived(rt.at[2, slots[i], BZ_ROWS if h else A_ROWS], r_f + 2 * i + h)
        columns(2, blocks, begin=0 in blocks, end=3 in blocks)


def per_device(activations, out_grads, in_basis, out_basis):
    bf = jnp.bfloat16
    vmem = pl.BlockSpec(memory_space=pltpu.VMEM)
    pads = ((0, 0), (0, 512))
    own = jnp.concatenate(
        [out_grads, out_basis.T, jnp.pad(activations, pads), jnp.pad(in_basis.T, pads)], axis=0)
    return pl.pallas_call(
        kernel,
        out_shape=jax.ShapeDtypeStruct((512, 1024), jnp.float32),
        in_specs=[vmem],
        out_specs=vmem,
        scratch_shapes=[
            pltpu.VMEM((NY, NH, 2, XROWS, 512), bf),
            pltpu.VMEM((NX, 128, 1024), bf),
            pltpu.VMEM((NL, 64, 1024), bf),
            pltpu.VMEM((NX, NL, 256, 512), bf),
            pltpu.VMEM((512, 512), bf),
            pltpu.VMEM((NL, 512, 512), bf),
            pltpu.VMEM((NL, 512, 512), bf),
            pltpu.VMEM((2, 512, 256), jnp.float32),
            pltpu.SemaphoreType.DMA((110,)),
            pltpu.SemaphoreType.DMA((100,)),
            pltpu.SemaphoreType.DMA((3,)),
        ],
        compiler_params=pltpu.CompilerParams(
            collective_id=0, has_side_effects=True, vmem_limit_bytes=48 * 2**20),
        cost_estimate=pl.CostEstimate(
            flops=6 * 10**9, bytes_accessed=4 * 2**20, transcendentals=0),
        name="gather_and_scale",
    )(own)


def solution(mesh):
    in_specs = (P("fsdp", "rep"), P("rep", "fsdp"), P("rep", "fsdp"), P("fsdp", "rep"))
    out_specs = P("rep", "fsdp")
    return jax.shard_map(
        per_device, mesh=mesh, in_specs=in_specs, out_specs=out_specs, check_vma=False
    )
```

```python
import functools

import jax
import jax.numpy as jnp
from jax import lax
from jax.experimental import pallas as pl
from jax.experimental.pallas import tpu as pltpu
from jax.sharding import PartitionSpec as P

MESH = pl.DeviceIdType.MESH
DAMPING = 0.001
TOKENS = 2048
NX, NL, NH, NY = 4, 4, 2, 8
XROWS = 80
WROWS = 48
A_ROWS = pl.ds(0, 128)
B_ROWS = pl.ds(128, 128)
BZ_ROWS = pl.ds(128, 128 - WROWS)
W_ROWS = pl.ds(256 - WROWS, WROWS)
LEFT, RIGHT = pl.ds(0, 256), pl.ds(256, 256)
NT = (((1,), (1,)), ((), ()))
END_ORDER = (
    "L1", "L2", "Y01", "G1", "G2", "L3", "Z4", "B0", "B1", "Y02", "GA", "Y03", "B2", "GB", "XZ",
    "WX", "T0A", "Y11", "WF", "T0B", "T1A", "WZ", "Y12", "T1B", "F0A", "F0B", "T2A", "F1B",
    "Y13", "F1A", "Y04", "Y14", "T2B", "F2A", "F3A", "RX", "F2B", "V1", "V0", "F3B", "C0", "V2",
)
INNER_ORDER = (
    "L1", "L2", "B1", "B0", "G2", "L3", "G1", "Z4", "Y01", "B2", "GA", "Y02", "GB", "XZ", "WX",
    "Y03", "T0A", "T1A", "Y11", "WF", "T1B", "T0B", "F0A", "T2A", "Y12", "WZ", "Y13", "Y04",
    "T2B", "F2A", "F2B", "V0", "Y14", "F0B", "F1A", "F1B", "V1", "F3A", "V2", "RX", "F3B", "C0",
)


def dot_nt(a, b):
    return lax.dot_general(a, b, NT, preferred_element_type=jnp.float32)


def square(a):
    wide = a.astype(jnp.float32)
    return (wide * wide).astype(jnp.bfloat16)


def slot_of(x):
    return (x % 2) * 2 + x // 2


def along_plus(i, h):
    return (h + i) % 2 == 0


def kernel(own_ref, out, xbuf, gbuf, bbuf, rt, bx, rx, sx, acc, sq, send_sem, recv_sem, own_sem, level):
    rep, f = lax.axis_index("rep"), lax.axis_index("fsdp")
    x, zl = rep // NL, rep % NL
    zh, y, c = f // 16, (f // 2) % NY, f % 2
    inner = (zl + 1) // 2 % 2
    xp = (((x + 1) % NX) * NL + zl, f)
    xm = (((x + 3) % NX) * NL + zl, f)
    arrivals = (zl + 1 - 2 * (zl % 2), 2 - zl // 2, 3 - 3 * (zl // 2))
    slots = (zl,) + arrivals
    nb1 = (x * NL + arrivals[0], f)
    nb2 = (x * NL + (3 - zl), f)
    z = zh * NL + zl
    zp, zm = (
        (x * NL + (z + d) % 8 % NL, (z + d) % 8 // NL * 16 + y * 2 + c) for d in (1, 7))
    yp = (rep, zh * 16 + ((y + 1) % NY) * 2 + c)
    ym = (rep, zh * 16 + ((y + 7) % NY) * 2 + c)
    z4 = (rep, (1 - zh) * 16 + y * 2 + c)
    co = (rep, f + 1 - 2 * c)
    ys = [((y + d) % NY) % 4 * 2 + ((y + d) % NY) // 4 for d in range(NY)]
    g_own, g_m, g_p, g_2 = (slot_of((x + d) % NX) for d in (0, 3, 1, 2))
    pair = zl // 2 * 2
    hzs = (zh, 1 - zh)

    count = [0]

    def sems(n):
        count[0] += n
        return count[0] - n

    r_g, r_b, r_zh = sems(6), sems(2 * NL), sems(1)
    r_y, r_c, r_co = sems(16), sems(16), sems(2)
    r_t, r_x, r_f = sems(2 * NL), sems(4 * NL), sems(2 * NL)
    r_w, r_v = sems(4), sems(NL)

    def copy(src, dst, s, r, dev):
        return pltpu.make_async_remote_copy(
            src_ref=src, dst_ref=dst, send_sem=send_sem.at[s], recv_sem=recv_sem.at[r],
            device_id=dev, device_id_type=MESH)

    def arrived(dst, r):
        copy(dst, dst, 0, r, xp).wait_recv()

    partners = (xp, xm, zp, zm, yp, ym, co)
    barrier = pltpu.get_barrier_semaphore()
    for dev in partners:
        pl.semaphore_signal(barrier, inc=1, device_id=dev, device_id_type=MESH)

    x_own = xbuf.at[ys[0], zh, c]
    load = [
        pltpu.make_async_copy(own_ref.at[pl.ds(0, 128)], gbuf.at[g_own], own_sem.at[0]),
        pltpu.make_async_copy(own_ref.at[pl.ds(128, 64)], bbuf.at[zl], own_sem.at[1]),
        pltpu.make_async_copy(own_ref.at[pl.ds(192, XROWS), pl.ds(0, 512)], x_own, own_sem.at[2]),
    ]
    for cp in load:
        cp.start()
    for cp in load:
        cp.wait()
    pl.semaphore_wait(barrier, len(partners))

    def tell(k):
        pl.semaphore_signal(level.at[k - 1], inc=1, device_id=zm, device_id_type=MESH)

    tell(1)

    def rot_x(t, _):
        data = xbuf[pl.ds(t * 2, 2), :, :, pl.ds(0, 64), :].reshape(512, 512)
        turned = dot_nt(bx[...], data).astype(jnp.bfloat16)
        rx[t] = turned
        sx[t] = square(turned)
        return 0

    def columns(dx, blocks, begin=True, end=True):
        cols = [
            pl.ds(pl.multiple_of((x + dx) % NX * 256 + p * 128, 128), 128)
            for p in (zl // 2, 1 - zl // 2)]

        def block(i):
            halves = [rt[dx, slots[i], A_ROWS, :], rt[dx, slots[i], B_ROWS, :]]
            return jnp.concatenate(halves if i < 2 else halves[::-1], axis=0)

        for i in blocks:
            sq[i] = square(block(i))

        def rows(m, _):
            here = pl.ds(pl.multiple_of(m * 256, 256), 256)
            if begin:
                grad = jnp.zeros((256, 256), jnp.float32)
                scale = jnp.zeros((256, 256), jnp.float32)
            else:
                grad, scale = acc[0, here, :], acc[1, here, :]
            for i in blocks:
                t = slots[i]
                grad += dot_nt(rx[t, here, :], block(i))
                scale += dot_nt(sx[t, here, :], sq[i])
            if end:
                result = (grad / TOKENS) / (scale / TOKENS + DAMPING)
                out[here, cols[0]] = result[:, :128]
                out[here, cols[1]] = result[:, 128:]
            else:
                acc[0, here, :] = grad
                acc[1, here, :] = scale
            return 0

        lax.fori_loop(0, 2, rows, 0)

    def program(inside, order, finish):
        count = [0]

        def send(src, dst, r, dev):
            cp = copy(src, dst, count[0], r, dev)
            count[0] += 1
            if finish:
                cp.wait_send()
            else:
                cp.start()

        def recv(dst, r):
            if not finish:
                arrived(dst, r)

        def pass_on(ref, r, dev):
            send(ref, ref, r, dev)

        def own_z(ref, r):
            pass_on(ref, r, nb1)
            if inside:
                pass_on(ref, r, nb2)

        def next_z(e, ref, r):
            if inside:
                pass_on(ref, r, nb2 if e == 0 else nb1)

        def b_part(s, q):
            return bbuf.at[s, :, pl.ds(q * 512, 512)]

        def x_sends(i, h):
            s, r = slots[i], r_x + 4 * i + 2 * h
            rows = BZ_ROWS if h else A_ROWS
            send(rt.at[0, s, rows], rt.at[3, s, rows], r, xp)
            send(rt.at[0, s, rows], rt.at[1, s, rows], r + 1, xm)

        def tile(h):
            first = pair if h == 0 else 2 - pair
            rows = B_ROWS if h else A_ROWS
            if not finish:
                basis = bbuf[pl.ds(first, 2)].reshape(128, 1024)
                turned = dot_nt(basis, gbuf[...].reshape(512, 1024))
                rt[0, zl, rows, :] = turned.astype(jnp.bfloat16)
            own_z(rt.at[0, zl, rows], r_t + 2 * zl + h)
            x_sends(0, h)

        def y_event(flow, k):
            for way in range(2):
                src = xbuf.at[ys[(8 - k) % 8 if way == 0 else k], hzs[flow], c]
                to = yp if way == 0 else ym
                half = src.at[pl.ds(0, XROWS), LEFT if way == 0 else RIGHT]
                if k == 4:
                    src = half
                r = (flow * 4 + k - 1) * 2 + way
                recv(src, r_y + r)
                if k < 3:
                    pass_on(src, r_y + r + 2, to)
                elif k == 3:
                    pass_on(half, r_y + r + 2, to)
                pass_on(src, r_c + r, co)

        def event(name):
            kind = name[0]
            if kind == "L":
                if not finish:
                    pl.semaphore_wait(level.at[int(name[1]) - 1], 1)
                    if name != "L3":
                        tell(int(name[1]) + 1)
            elif name == "Z4":
                pass_on(x_own, r_zh, z4)
            elif name == "XZ":
                far = xbuf.at[ys[0], 1 - zh, c]
                recv(far, r_zh)
                pass_on(far, r_y + 8, yp)
                pass_on(far, r_y + 9, ym)
                pass_on(far, r_co + 1, co)
            elif kind == "Y":
                y_event(int(name[1]), int(name[2]))
            elif kind == "B":
                e = int(name[1])
                s = arrivals[e]
                for q in range(2):
                    recv(b_part(s, q), r_b + 2 * s + q)
                    next_z(e, b_part(s, q), r_b + 2 * s + q)
            elif name == "G1":
                recv(gbuf.at[g_m, h0], r_g)
                pass_on(gbuf.at[g_m, h0], r_g + 4, xp)
            elif name == "G2":
                recv(gbuf.at[g_p, h1], r_g + 1)
                pass_on(gbuf.at[g_p, h1], r_g + 5, xm)
            elif name == "GA":
                recv(gbuf.at[g_m, h1], r_g + 2)
                recv(gbuf.at[g_p, h0], r_g + 3)
                recv(gbuf.at[g_2, h0], r_g + 4)
                recv(gbuf.at[g_2, h1], r_g + 5)
                tile(0)
            elif name == "GB":
                tile(1)
            elif name == "WX":
                send(rt.at[0, zl, W_ROWS], rt.at[3, zl, W_ROWS], r_w, xp)
                send(rt.at[0, zl, W_ROWS], rt.at[1, zl, W_ROWS], r_w + 1, xm)
            elif name == "WF":
                recv(rt.at[3, zl, W_ROWS], r_w)
                send(rt.at[3, zl, W_ROWS, LEFT], rt.at[2, zl, W_ROWS, LEFT], r_w + 2, xp)
                recv(rt.at[1, zl, W_ROWS], r_w + 1)
                send(rt.at[1, zl, W_ROWS, RIGHT], rt.at[2, zl, W_ROWS, RIGHT], r_w + 3, xm)
            elif name == "WZ":
                recv(rt.at[2, zl, W_ROWS, LEFT], r_w + 2)
                recv(rt.at[2, zl, W_ROWS, RIGHT], r_w + 3)
                own_z(rt.at[pl.ds(1, 3), zl, W_ROWS], r_v + zl)
            elif kind == "V":
                e = int(name[1])
                s = arrivals[e]
                part = rt.at[pl.ds(1, 3), s, W_ROWS]
                recv(part, r_v + s)
                next_z(e, part, r_v + s)
            elif kind == "T":
                e, h = int(name[1]), "AB".index(name[2])
                s = arrivals[e]
                part = rt.at[0, s, B_ROWS if h else A_ROWS]
                recv(part, r_t + 2 * s + h)
                next_z(e, part, r_t + 2 * s + h)
                x_sends(e + 1, h)
            elif kind == "F":
                i, h = int(name[1]), "AB".index(name[2])
                s, rows, r = slots[i], BZ_ROWS if h else A_ROWS, r_x + 4 * i + 2 * h
                if along_plus(i, h):
                    recv(rt.at[3, s, rows], r)
                    send(rt.at[3, s, rows], rt.at[2, s, rows], r_f + 2 * i + h, xp)
                else:
                    recv(rt.at[1, s, rows], r + 1)
                    send(rt.at[1, s, rows], rt.at[2, s, rows], r_f + 2 * i + h, xm)
            elif finish:
                pass
            elif name == "RX":
                for flow in range(2):
                    recv(xbuf.at[ys[0], hzs[flow], 1 - c], r_co + flow)
                    for k in range(1, 5):
                        for way in range(2):
                            dst = xbuf.at[ys[(8 - k) % 8 if way == 0 else k], hzs[flow], 1 - c]
                            if k == 4:
                                dst = dst.at[pl.ds(0, XROWS), LEFT if way == 0 else RIGHT]
                            recv(dst, r_c + (flow * 4 + k - 1) * 2 + way)
                for i in range(32):
                    ih, iy, ic = i // 16, i // 2 % 8, i % 2
                    bx[pl.ds(i * 16, 16), :] = xbuf[iy % 4 * 2 + iy // 4, ih, ic, pl.ds(64, 16), :]
                lax.fori_loop(0, NL, rot_x, 0)
            elif name == "C0":
                columns(0, range(NL))

        h0, h1 = pl.ds(0, 64), pl.ds(64, 64)
        pass_on(gbuf.at[g_own, h0], r_g, xp)
        pass_on(gbuf.at[g_own, h1], r_g + 1, xm)
        for q in range(2):
            own_z(b_part(zl, q), r_b + 2 * zl + q)
        pass_on(x_own, r_y, yp)
        pass_on(x_own, r_y + 1, ym)
        pass_on(x_own, r_co, co)
        pass_on(gbuf.at[g_own, h1], r_g + 2, xp)
        pass_on(gbuf.at[g_own, h0], r_g + 3, xm)
        for name in order:
            event(name)

    def both(finish):
        pl.when(inner == 0)(lambda: program(False, END_ORDER, finish))
        pl.when(inner == 1)(lambda: program(True, INNER_ORDER, finish))

    both(False)
    for i in range(NL):
        for h in range(2):
            if along_plus(i, h):
                arrived(rt.at[1, slots[i], BZ_ROWS if h else A_ROWS], r_x + 4 * i + 2 * h + 1)
    columns(1, range(NL))
    for i in range(NL):
        for h in range(2):
            if not along_plus(i, h):
                arrived(rt.at[3, slots[i], BZ_ROWS if h else A_ROWS], r_x + 4 * i + 2 * h)
    columns(3, range(NL))
    for blocks in ((0, 1, 2), (3,)):
        for i in blocks:
            for h in range(2):
                arrived(rt.at[2, slots[i], BZ_ROWS if h else A_ROWS], r_f + 2 * i + h)
        columns(2, blocks, begin=0 in blocks, end=3 in blocks)
    both(True)


def per_device(activations, out_grads, in_basis, out_basis):
    bf = jnp.bfloat16
    vmem = pl.BlockSpec(memory_space=pltpu.VMEM)
    pads = ((0, 0), (0, 512))
    own = jnp.concatenate(
        [out_grads, out_basis.T, jnp.pad(activations, pads), jnp.pad(in_basis.T, pads)], axis=0)
    return pl.pallas_call(
        kernel,
        out_shape=jax.ShapeDtypeStruct((512, 1024), jnp.float32),
        in_specs=[vmem],
        out_specs=vmem,
        scratch_shapes=[
            pltpu.VMEM((NY, NH, 2, XROWS, 512), bf),
            pltpu.VMEM((NX, 128, 1024), bf),
            pltpu.VMEM((NL, 64, 1024), bf),
            pltpu.VMEM((NX, NL, 256, 512), bf),
            pltpu.VMEM((512, 512), bf),
            pltpu.VMEM((NL, 512, 512), bf),
            pltpu.VMEM((NL, 512, 512), bf),
            pltpu.VMEM((2, 512, 256), jnp.float32),
            pltpu.VMEM((NL, 256, 512), bf),
            pltpu.SemaphoreType.DMA((110,)),
            pltpu.SemaphoreType.DMA((100,)),
            pltpu.SemaphoreType.DMA((3,)),
            pltpu.SemaphoreType.REGULAR((3,)),
        ],
        compiler_params=pltpu.CompilerParams(
            collective_id=0, has_side_effects=True, vmem_limit_bytes=48 * 2**20),
        cost_estimate=pl.CostEstimate(
            flops=6 * 10**9, bytes_accessed=4 * 2**20, transcendentals=0),
        name="gather_and_scale",
    )(own)


def solution(mesh):
    in_specs = (P("fsdp", "rep"), P("rep", "fsdp"), P("rep", "fsdp"), P("fsdp", "rep"))
    out_specs = P("rep", "fsdp")
    return jax.shard_map(
        per_device, mesh=mesh, in_specs=in_specs, out_specs=out_specs, check_vma=False
    )
```
